256 devices in a mesh: row: 8 (over x, core), col: 32 (over z, y).
Axes of the slice: x: 4, y: 4, z: 8, core: 2. Of those that a mesh axis runs over, the one named last changes fastest.
Arguments:
- tokens: bfloat16 [128, 8192], P('row', 'col'), may hold values from -7 to 7
- cotangent: bfloat16 [128, 8192], P('row', 'col'), may hold values from -7 to 7
- gate_weight: bfloat16 [8192, 28672], P('col', 'row'), may hold values from -0.0625 to 0.0625
- up_weight: bfloat16 [8192, 28672], P('col', 'row'), may hold values from -0.0625 to 0.0625
- down_weight: bfloat16 [28672, 8192], P('row', 'col'), may hold values from -0.03125 to 0.03125
- coefficients: float32 [2, 1000], replicated, may hold values from -4 to 4
- spectral_rows: int32 [2, 1000], replicated, may hold values from 0 to 28671, as said below
- spectral_cols: int32 [2, 1000], replicated, may hold values from 0 to 28671, as said below
- adam_first: float32 [2, 1000], replicated, may hold values from -0.0234375 to 0.0234375
- adam_second: float32 [2, 1000], replicated, may hold values from 2e-07 to 5e-06
Outputs:
- mixed: bfloat16 [128, 8192], P('row', 'col')
- adam_step: float32 [2, 1000], replicated
The draws below stay inside these ranges and needn't reach their ends.
Inputs may be any that keep to these rules, and one draw needn't show every extreme that they name: `spectral_rows`: row 0 lies below 8192, row 1 below 28672. `spectral_cols`: row 0 lies below 28672, row 1 below 8192.
All inputs are finite; a program needn't handle non-finite values.
Results may differ from the reference program's by a relative error of at most 0.015.
Values may be sent and summed in bfloat16 or wider, within the bound.
No kernel may reach another device: no remote copies, remote signals or barrier semaphores. Data moves between devices by JAX's collectives and lax.ppermute only.
A program may use at most 128 MiB of HBM per device.

```python
import math
import jax
import jax.numpy as jnp
from jax import lax

D = 8192
FF = 28672
N_COEF = 1000
TOKENS = 128
ADAM_STEP = 3


def column_ramp(width, rise):
    index = jnp.arange(width, dtype=jnp.float32)
    return jnp.exp(jnp.log(rise) * (index / (width - 1) - 0.5))


def ramped_field(key, rows, width):
    values = jnp.clip(jax.random.normal(key, (rows, width), jnp.float32), -4.0, 4.0) * column_ramp(width, 3.0)
    return values


def draw_tokens(key, part):
    key = jax.random.fold_in(key, 11)
    return ramped_field(key, TOKENS, D).astype(jnp.bfloat16)


def draw_cotangent(key, part):
    key = jax.random.fold_in(key, 12)
    return ramped_field(key, TOKENS, D).astype(jnp.bfloat16)


def draw_spectral_rows(key, part):
    key = jax.random.fold_in(key, 21)
    limits = jnp.array([[D], [FF]], dtype=jnp.int32)
    return jax.random.randint(key, (2, N_COEF), 0, limits, dtype=jnp.int32)


def draw_spectral_cols(key, part):
    key = jax.random.fold_in(key, 22)
    limits = jnp.array([[FF], [D]], dtype=jnp.int32)
    return jax.random.randint(key, (2, N_COEF), 0, limits, dtype=jnp.int32)


def block_scale(own_key, shape, cuts, least, high):
    gain = 1.0
    for axis_at, shards_of in cuts:
        draws = jax.random.uniform(jax.random.fold_in(jax.random.fold_in(own_key, 6), axis_at), (shards_of,), jnp.float32, least / len(cuts), high / len(cuts))
        gain = gain * jnp.repeat(jnp.exp(draws), shape[axis_at] // shards_of).reshape((-1,) + (1,) * (len(shape) - 1 - axis_at))
    return gain


def gaussian(own_key, dims, scale, bound, pieces=(), held_as=jnp.bfloat16):
    drawn = jax.random.normal(own_key, dims, jnp.float32) * scale
    if len(pieces) > 0:
        drawn = block_scale(own_key, dims, pieces, -0.22, 0.18) * drawn
    return jnp.clip(drawn, min=-bound, max=bound).astype(held_as)


def setup_inputs(seed: int = 0) -> dict:
    seeds = jax.random.split(jax.random.key(seed), 11)
    tokens = draw_tokens(jax.random.fold_in(seeds[10], 71), 0)
    cotangent = draw_cotangent(jax.random.fold_in(seeds[10], 71), 0)
    gate_weight = gaussian(seeds[2], (D, FF), D ** -0.5, 0.0625, ((0, 32), (1, 8)))
    up_weight = gaussian(seeds[3], (D, FF), D ** -0.5, 0.0625, ((0, 32), (1, 8)))
    down_weight = gaussian(seeds[4], (FF, D), FF ** -0.5, 0.03125, ((0, 8), (1, 32)))
    coefficients = gaussian(seeds[5], (2, N_COEF), 1.0, 4.0, (), jnp.float32)
    spectral_rows = draw_spectral_rows(jax.random.fold_in(seeds[10], 71), 0)
    spectral_cols = draw_spectral_cols(jax.random.fold_in(seeds[10], 71), 0)
    adam_first = gaussian(seeds[8], (2, N_COEF), 0.004, 0.0234375, (), jnp.float32)
    adam_second = jnp.clip(jnp.exp(jax.random.uniform(seeds[9], (2, N_COEF), jnp.float32, math.log(2.0000000233721948e-07), math.log(4.999999873689376e-06))), 2.0000000233721948e-07, 4.999999873689376e-06)
    return dict(tokens=tokens, cotangent=cotangent, gate_weight=gate_weight, up_weight=up_weight, down_weight=down_weight, coefficients=coefficients, spectral_rows=spectral_rows, spectral_cols=spectral_cols, adam_first=adam_first, adam_second=adam_second)


two_pi = 6.283185307179586

def basis_table(positions, width, sign):
    index = jnp.arange(width, dtype=jnp.int32)
    phase = positions[:, None] * index[None, :] % width
    angle = phase.astype(jnp.float32) * (two_pi / width)
    return jnp.concatenate([jnp.cos(angle), sign * jnp.sin(angle)], axis=0).astype(jnp.bfloat16)

def against(left, table):
    return lax.dot_general(left, table, (((1,), (1,)), ((), ())), preferred_element_type=jnp.float32)

def matmul(left, right):
    return jnp.dot(left, right, preferred_element_type=jnp.float32)

def reference(tokens, cotangent, gate_weight, up_weight, down_weight, coefficients, spectral_rows, spectral_cols, adam_first, adam_second):
    scale_up = 1.0 / math.sqrt(2.0 * D * N_COEF)
    scale_down = 1.0 / math.sqrt(2.0 * FF * N_COEF)
    left_up = basis_table(spectral_rows[0], D, 1.0)
    right_up = basis_table(spectral_cols[0], FF, -1.0)
    left_down = basis_table(spectral_rows[1], FF, 1.0)
    right_down = basis_table(spectral_cols[1], D, -1.0)
    coef_up = jnp.concatenate([coefficients[0], coefficients[0]]) * scale_up
    coef_down = jnp.concatenate([coefficients[1], coefficients[1]]) * scale_down
    gate = matmul(tokens, gate_weight)
    proj_up = against(tokens, left_up)
    weighted_up = (proj_up * coef_up).astype(jnp.bfloat16)
    up_value = matmul(tokens, up_weight) + matmul(weighted_up, right_up)
    activated = jax.nn.silu(gate).astype(jnp.bfloat16)
    hidden = (activated.astype(jnp.float32) * up_value).astype(jnp.bfloat16)
    proj_down = against(hidden, left_down)
    weighted_down = (proj_down * coef_down).astype(jnp.bfloat16)
    mixed = (matmul(hidden, down_weight) + matmul(weighted_down, right_down)).astype(jnp.bfloat16)
    back_down = against(cotangent, right_down)
    down_pairs = lax.optimization_barrier(jnp.sum(proj_down * back_down, axis=0))
    grad_down = scale_down * (down_pairs[:N_COEF] + down_pairs[N_COEF:])
    weighted_back = (back_down * coef_down).astype(jnp.bfloat16)
    dhidden = against(cotangent, down_weight) + matmul(weighted_back, left_down)
    dup = (dhidden * activated.astype(jnp.float32)).astype(jnp.bfloat16)
    back_up = against(dup, right_up)
    up_pairs = lax.optimization_barrier(jnp.sum(proj_up * back_up, axis=0))
    grad_up = scale_up * (up_pairs[:N_COEF] + up_pairs[N_COEF:])
    grads = jnp.stack([grad_up, grad_down])
    norm_value = jnp.sqrt(jnp.sum(grads * grads))
    clipped = grads * jnp.minimum(1.0, 1.0 / (norm_value + 1e-06))
    first = 0.9 * adam_first + 0.1 * clipped
    second = 0.999 * adam_second + 0.001 * clipped * clipped
    adam_step = first / (1.0 - 0.9 ** ADAM_STEP) / (jnp.sqrt(second / (1.0 - 0.999 ** ADAM_STEP)) + 1e-08)
    return (mixed, adam_step)
```

```python
import math

import jax
import jax.numpy as jnp
from jax import lax
from jax.experimental import pallas as pl
from jax.experimental.pallas import tpu as pltpu
from jax.sharding import Mesh
from jax.sharding import PartitionSpec as P

D = 8192
FF = 28672
N_COEF = 1000
ADAM_STEP = 3
PAD = 1024
SCALE_UP = 1.0 / math.sqrt(2.0 * D * N_COEF)
SCALE_DOWN = 1.0 / math.sqrt(2.0 * FF * N_COEF)
TWO_PI = 6.283185307179586

F32 = jnp.float32
BF16 = jnp.bfloat16
LOW = 8
MID = 16
SPAN = LOW * MID

PLANE = ("x", "core")
VMEM = pl.BlockSpec(memory_space=pltpu.VMEM)


def params(mib):
    return pltpu.CompilerParams(vmem_limit_bytes=mib << 20)


def phases(freq, first, blocks, width):
    rows = -(-(LOW + MID + blocks) // 8) * 8
    index = jnp.concatenate(
        [
            jnp.arange(LOW, dtype=jnp.int32),
            LOW * jnp.arange(MID, dtype=jnp.int32),
            first + SPAN * jnp.arange(blocks, dtype=jnp.int32),
            jnp.zeros(rows - LOW - MID - blocks, jnp.int32),
        ]
    )
    phase = index[:, None] * freq[None, :] % width
    angle = phase.astype(F32) * (TWO_PI / width)
    return jnp.stack([jnp.cos(angle), jnp.sin(angle)])


def span_table(cos, sin):
    low_cos, low_sin = cos[:LOW], sin[:LOW]
    out_cos, out_sin = [], []
    for k in range(MID):
        a, b = cos[LOW + k : LOW + k + 1], sin[LOW + k : LOW + k + 1]
        out_cos.append(a * low_cos - b * low_sin)
        out_sin.append(b * low_cos + a * low_sin)
    return jnp.concatenate(out_cos, axis=0), jnp.concatenate(out_sin, axis=0)


def turned(cos, sin, span_cos, span_sin):
    return cos * span_cos - sin * span_sin, sin * span_cos + cos * span_sin


def against(left, table):
    return lax.dot_general(
        left, table, (((1,), (1,)), ((), ())), preferred_element_type=F32
    )


def matmul(left, right):
    return jnp.dot(left, right, preferred_element_type=F32)


def split(value):
    high = value.astype(BF16)
    return high, (value - high.astype(F32)).astype(BF16)


def first_kernel(x_ref, own_ref, gate_ref, up_ref, down_ref, base_ref, out_ref):
    quarter = pl.program_id(0)
    wide = gate_ref.shape[1]
    feats = gate_ref.shape[0]
    tokens = x_ref[:, :feats]
    cotangent = x_ref[:, feats:]
    out_ref[0, :, :wide] = matmul(tokens, gate_ref[...]).astype(BF16)
    out_ref[0, :, wide : 2 * wide] = matmul(tokens, up_ref[...]).astype(BF16)
    out_ref[0, :, 2 * wide : 3 * wide] = against(cotangent, down_ref[...]).astype(BF16)
    cos, sin = base_ref[0, 0], base_ref[0, 1]
    span_cos, span_sin = span_table(cos, sin)
    sign = jnp.where(quarter == 3, -1.0, 1.0).astype(F32)
    pieces = []
    for block in range(feats // SPAN):
        at = LOW + MID + block
        c, s = turned(cos[at : at + 1], sin[at : at + 1], span_cos, span_sin)
        pieces.append(jnp.where(quarter % 2 == 0, c, sign * s).astype(BF16))
    table = jnp.concatenate(pieces, axis=0)
    out_ref[0, :, 3 * wide :] = matmul(own_ref[...], table).astype(BF16)


def middle_kernel(
    sums_ref, proj_ref, coef_ref, base_ref, out_ref, table_up, table_down
):
    wide = table_up.shape[0]
    rows = sums_ref.shape[1]

    def summed(first, last):
        total = sums_ref[0, :, first:last].astype(F32)
        for z in range(1, sums_ref.shape[0]):
            total += sums_ref[z, :, first:last].astype(F32)
        return total

    def kind(y):
        return jnp.concatenate(
            [proj_ref[r, y].astype(F32) for r in range(proj_ref.shape[0])], axis=1
        )

    for which, table, sign in ((0, table_up, -1.0), (1, table_down, 1.0)):
        for tile in range(PAD // SPAN):
            lanes = slice(tile * SPAN, (tile + 1) * SPAN)
            cos, sin = base_ref[which, 0, :, lanes], base_ref[which, 1, :, lanes]
            span_cos, span_sin = span_table(cos, sin)
            for block in range(wide // SPAN):
                at = LOW + MID + block
                c, s = turned(cos[at : at + 1], sin[at : at + 1], span_cos, span_sin)
                units = slice(block * SPAN, (block + 1) * SPAN)
                table[units, lanes] = c.astype(BF16)
                table[units, PAD + tile * SPAN : PAD + (tile + 1) * SPAN] = (
                    sign * s
                ).astype(BF16)

    proj_up = jnp.concatenate([kind(0), kind(1)], axis=1)
    back_down = jnp.concatenate([kind(2), kind(3)], axis=1)
    coef_up = jnp.concatenate([coef_ref[0:1], coef_ref[0:1]], axis=1) * SCALE_UP
    coef_down = jnp.concatenate([coef_ref[1:2], coef_ref[1:2]], axis=1) * SCALE_DOWN
    weighted_up = (proj_up * coef_up).astype(BF16)
    weighted_back = (back_down * coef_down).astype(BF16)
    gate = summed(0, wide)
    up = summed(wide, 2 * wide) + against(weighted_up, table_up[...])
    dhidden = summed(2 * wide, 3 * wide) + against(weighted_back, table_down[...])
    activated = (gate / (1.0 + jnp.exp(-gate))).astype(BF16).astype(F32)
    hidden = (activated * up).astype(BF16)
    dup = (dhidden * activated).astype(BF16)
    back_up = matmul(dup, table_up[...])
    proj_down = matmul(hidden, table_down[...])
    up_pairs = jnp.sum(proj_up * back_up, axis=0, keepdims=True)
    down_pairs = jnp.sum(proj_down * back_down, axis=0, keepdims=True)
    grad_up = SCALE_UP * (up_pairs[:, :PAD] + up_pairs[:, PAD:])
    grad_down = SCALE_DOWN * (down_pairs[:, :PAD] + down_pairs[:, PAD:])
    grads = jnp.concatenate(
        [g[:, k * SPAN : (k + 1) * SPAN] for g in (grad_up, grad_down) for k in range(PAD // SPAN)],
        axis=0,
    )
    high, low = split(grads)
    for z in range(out_ref.shape[0]):
        out_ref[z, :, :wide] = hidden
        out_ref[z, :, wide : wide + SPAN] = high
        out_ref[z, :, wide + SPAN :] = low


def regroup_kernel(in_ref, out_ref):
    peers, rows, _ = in_ref.shape
    wide = out_ref.shape[2]
    grads = jnp.zeros((rows, SPAN), F32)
    for z in range(peers):
        grads += in_ref[z, :, wide : wide + SPAN].astype(F32)
        grads += in_ref[z, :, wide + SPAN :].astype(F32)
    high, low = split(grads)
    rest = jnp.zeros((rows, wide - 2 * SPAN), BF16)
    for y in range(out_ref.shape[0]):
        for z in range(peers):
            out_ref[y, z * rows : (z + 1) * rows, :] = in_ref[z, :, :wide]
        out_ref[y, peers * rows :, :SPAN] = high
        out_ref[y, peers * rows :, SPAN : 2 * SPAN] = low
        out_ref[y, peers * rows :, 2 * SPAN :] = rest


def last_kernel(
    hidden_ref, down_ref, coef_ref, base_ref, base_out_ref, out_ref, total, table
):
    step = pl.program_id(0)
    quarters, _, wide = hidden_ref.shape
    tokens, feats = total.shape

    @pl.when(step == 0)
    def _():
        value = matmul(hidden_ref[0, :tokens, :], down_ref[:wide, :])
        for y in range(1, quarters):
            value += matmul(
                hidden_ref[y, :tokens, :], down_ref[y * wide : (y + 1) * wide, :]
            )
        total[...] = value

    cos, sin = base_ref[0], base_ref[1]
    span_cos, span_sin = span_table(cos, sin)
    for block in range(table.shape[0] // SPAN):
        at = LOW + MID + block
        c, s = turned(cos[at : at + 1], sin[at : at + 1], span_cos, span_sin)
        units = slice(block * SPAN, (block + 1) * SPAN)
        table[units, :SPAN] = c.astype(BF16)
        table[units, SPAN:] = s.astype(BF16)
    proj = matmul(hidden_ref[0, :tokens, :], table[:wide, :])
    for y in range(1, quarters):
        proj += matmul(hidden_ref[y, :tokens, :], table[y * wide : (y + 1) * wide, :])
    coef = jnp.concatenate([coef_ref[...], coef_ref[...]], axis=1)[1:2] * SCALE_DOWN
    weighted = (proj * coef).astype(BF16)
    cos, sin = base_out_ref[0], base_out_ref[1]
    span_cos, span_sin = span_table(cos, sin)
    pieces = []
    for block in range(feats // SPAN):
        at = LOW + MID + block
        c, s = turned(cos[at : at + 1], sin[at : at + 1], span_cos, span_sin)
        pieces.append(jnp.concatenate([c, -s], axis=1).astype(BF16))
    total[...] += against(weighted, jnp.concatenate(pieces, axis=0))

    @pl.when(step == pl.num_programs(0) - 1)
    def _():
        peers, rows, _ = out_ref.shape
        rows //= 2
        grads = jnp.zeros((rows, SPAN), F32)
        for y in range(quarters):
            grads += hidden_ref[y, tokens:, :SPAN].astype(F32)
            grads += hidden_ref[y, tokens:, SPAN : 2 * SPAN].astype(F32)
        high, low = split(grads)
        for r in range(peers):
            out_ref[r, :rows, :] = total[r * rows : (r + 1) * rows, :].astype(BF16)
            out_ref[r, rows:, :SPAN] = high
            out_ref[r, rows:, SPAN:] = low


def update_kernel(in_ref, first_ref, second_ref, mixed_ref, step_ref, scratch):
    peers, rows, _ = in_ref.shape
    rows //= 2
    mixed = jnp.zeros(mixed_ref.shape, F32)
    pieces = jnp.zeros((rows, SPAN), F32)
    for r in range(peers):
        mixed += in_ref[r, :rows, :].astype(F32)
        pieces += in_ref[r, rows:, :SPAN].astype(F32)
        pieces += in_ref[r, rows:, SPAN:].astype(F32)
    mixed_ref[...] = mixed.astype(BF16)
    per = PAD // SPAN
    for k in range(rows):
        at = k % per
        scratch[k // per : k // per + 1, at * SPAN : (at + 1) * SPAN] = pieces[k : k + 1]
    grads = scratch[:, :N_COEF]
    squares = jnp.sum(jnp.sum(grads * grads, axis=1, keepdims=True), axis=0, keepdims=True)
    norm_value = jnp.sqrt(squares)
    clipped = grads * jnp.minimum(1.0, 1.0 / (norm_value + 1e-06))
    first = 0.9 * first_ref[...] + 0.1 * clipped
    second = 0.999 * second_ref[...] + 0.001 * clipped * clipped
    step_ref[...] = (
        first / (1.0 - 0.9**ADAM_STEP) / (jnp.sqrt(second / (1.0 - 0.999**ADAM_STEP)) + 1e-08)
    )


def on_device(
    tokens,
    cotangent,
    gate_weight,
    up_weight,
    down_weight,
    coefficients,
    spectral_rows,
    spectral_cols,
    adam_first,
    adam_second,
):
    peers_row = lax.axis_size(PLANE)
    peers_z = lax.axis_size("z")
    peers_y = lax.axis_size("y")
    row_index = lax.axis_index(PLANE)
    z_index = lax.axis_index("z")
    y_index = lax.axis_index("y")
    own, feats = tokens.shape
    units = gate_weight.shape[1]
    wide = units // peers_y
    count = own * peers_row
    feat_first = (z_index * peers_y + y_index) * feats
    unit_first = row_index * units

    def exchange(value, axes):
        return lax.all_to_all(value, axes, 0, 0, tiled=True)

    def padded(values):
        return jnp.pad(values, (0, PAD - N_COEF))

    coefs = jnp.pad(coefficients, ((0, 0), (0, PAD - N_COEF)))
    lanes = row_index * SPAN
    own_left = lax.dynamic_slice_in_dim(padded(spectral_rows[0]), lanes, SPAN)
    own_right = lax.dynamic_slice_in_dim(padded(spectral_cols[1]), lanes, SPAN)
    base_own = jnp.stack(
        [
            phases(own_left, feat_first, feats // SPAN, D),
            phases(own_right, feat_first, feats // SPAN, D),
        ]
    )
    tile_first = unit_first + y_index * wide
    base_tile = jnp.stack(
        [
            phases(padded(spectral_cols[0]), tile_first, wide // SPAN, FF),
            phases(padded(spectral_rows[1]), tile_first, wide // SPAN, FF),
        ]
    )
    base_row = phases(padded(spectral_rows[1]), unit_first, units // SPAN, FF)
    base_out = phases(padded(spectral_cols[1]), feat_first, feats // SPAN, D)

    both = jnp.concatenate([tokens, cotangent], axis=1)
    both = jnp.broadcast_to(both[None], (peers_row, own, 2 * feats))
    both = exchange(both, PLANE).reshape(count, 2 * feats)

    block = 3 * wide + SPAN
    parts = pl.pallas_call(
        first_kernel,
        grid=(peers_y,),
        in_specs=[
            pl.BlockSpec((count, 2 * feats), lambda y: (0, 0)),
            pl.BlockSpec((count, feats), lambda y: (0, y // 2)),
            pl.BlockSpec((feats, wide), lambda y: (0, y)),
            pl.BlockSpec((feats, wide), lambda y: (0, y)),
            pl.BlockSpec((wide, feats), lambda y: (y, 0)),
            pl.BlockSpec((1,) + base_own.shape[1:], lambda y: (y // 2, 0, 0, 0)),
        ],
        out_specs=pl.BlockSpec((1, count, block), lambda y: (y, 0, 0)),
        out_shape=jax.ShapeDtypeStruct((peers_y, count, block), BF16),
        compiler_params=params(24),
    )(both, both, gate_weight, up_weight, down_weight, base_own)

    parts = exchange(parts, "y")
    parts = jnp.sum(parts.astype(F32), axis=0).astype(BF16)
    share = count // peers_z
    parts = exchange(parts.reshape(peers_z, share, block), "z")
    proj = jnp.sum(parts[:, :, 3 * wide :].astype(F32), axis=0).astype(BF16)
    proj = jnp.broadcast_to(proj[None], (peers_row * peers_y, share, SPAN))
    proj = exchange(proj, PLANE + ("y",)).reshape(peers_row, peers_y, share, SPAN)

    hidden = pl.pallas_call(
        middle_kernel,
        in_specs=[VMEM] * 4,
        out_specs=VMEM,
        out_shape=jax.ShapeDtypeStruct((peers_z, share, wide + 2 * SPAN), BF16),
        scratch_shapes=[pltpu.VMEM((wide, 2 * PAD), BF16)] * 2,
        compiler_params=params(24),
    )(parts, proj, coefs, base_tile)
    hidden = exchange(hidden, "z")
    hidden = pl.pallas_call(
        regroup_kernel,
        in_specs=[VMEM],
        out_specs=VMEM,
        out_shape=jax.ShapeDtypeStruct((peers_y, count + share, wide), BF16),
        compiler_params=params(16),
    )(hidden)
    hidden = exchange(hidden, "y")

    mixed = pl.pallas_call(
        last_kernel,
        grid=(PAD // SPAN,),
        in_specs=[
            pl.BlockSpec(hidden.shape, lambda i: (0, 0, 0)),
            pl.BlockSpec((units, feats), lambda i: (0, 0)),
            pl.BlockSpec((2, SPAN), lambda i: (0, i)),
            pl.BlockSpec(base_row.shape[:2] + (SPAN,), lambda i: (0, 0, i)),
            pl.BlockSpec(base_out.shape[:2] + (SPAN,), lambda i: (0, 0, i)),
        ],
        out_specs=pl.BlockSpec((peers_row, 2 * own, feats), lambda i: (0, 0, 0)),
        out_shape=jax.ShapeDtypeStruct((peers_row, 2 * own, feats), BF16),
        scratch_shapes=[
            pltpu.VMEM((count, feats), F32),
            pltpu.VMEM((units, 2 * SPAN), BF16),
        ],
        compiler_params=params(32),
    )(hidden, down_weight, coefs, base_row, base_out)
    mixed = exchange(mixed, PLANE)

    return pl.pallas_call(
        update_kernel,
        in_specs=[VMEM] * 3,
        out_specs=[VMEM] * 2,
        out_shape=[
            jax.ShapeDtypeStruct((own, feats), BF16),
            jax.ShapeDtypeStruct(adam_first.shape, F32),
        ],
        scratch_shapes=[pltpu.VMEM((2, PAD), F32)],
    )(mixed, adam_first, adam_second)


def solution(mesh):
    chips = Mesh(mesh.devices.reshape(4, 2, 8, 4), ("x", "core", "z", "y"))
    tiles = P(("x", "core"), ("z", "y"))
    weights = P(("z", "y"), ("x", "core"))
    placed = (tiles, tiles, weights, weights, tiles, P(), P(), P(), P(), P())
    return jax.shard_map(
        on_device, mesh=chips, in_specs=placed, out_specs=(tiles, P()), check_vma=False
    )
```

```python
import math

import jax
import jax.numpy as jnp
from jax import lax
from jax.experimental import pallas as pl
from jax.experimental.pallas import tpu as pltpu
from jax.sharding import Mesh
from jax.sharding import PartitionSpec as P

D = 8192
FF = 28672
N_COEF = 1000
ADAM_STEP = 3
PAD = 1024
SCALE_UP = 1.0 / math.sqrt(2.0 * D * N_COEF)
SCALE_DOWN = 1.0 / math.sqrt(2.0 * FF * N_COEF)
TWO_PI = 6.283185307179586

F32 = jnp.float32
BF16 = jnp.bfloat16
LOW = 8
MID = 16
SPAN = LOW * MID

PLANE = ("x", "core")
VMEM = pl.BlockSpec(memory_space=pltpu.VMEM)


def params(mib):
    return pltpu.CompilerParams(vmem_limit_bytes=mib << 20)


def waves(index, freq, width, axis):
    phase = index[..., None] * freq % width
    angle = phase.astype(F32) * (TWO_PI / width)
    return jnp.stack([jnp.cos(angle), jnp.sin(angle)], axis=axis)


def phases(freq, first, blocks, width):
    rows = -(-(LOW + MID + blocks) // 8) * 8
    index = jnp.concatenate(
        [
            jnp.arange(LOW, dtype=jnp.int32),
            LOW * jnp.arange(MID, dtype=jnp.int32),
            first + SPAN * jnp.arange(blocks, dtype=jnp.int32),
            jnp.zeros(rows - LOW - MID - blocks, jnp.int32),
        ]
    )
    return waves(index, freq, width, 0)


def span_table(cos, sin):
    low_cos, low_sin = cos[:LOW], sin[:LOW]
    out_cos, out_sin = [], []
    for k in range(MID):
        a, b = cos[LOW + k : LOW + k + 1], sin[LOW + k : LOW + k + 1]
        out_cos.append(a * low_cos - b * low_sin)
        out_sin.append(b * low_cos + a * low_sin)
    return jnp.concatenate(out_cos, axis=0), jnp.concatenate(out_sin, axis=0)


def turned(cos, sin, span_cos, span_sin):
    return cos * span_cos - sin * span_sin, sin * span_cos + cos * span_sin


def against(left, table):
    return lax.dot_general(
        left, table, (((1,), (1,)), ((), ())), preferred_element_type=F32
    )


def matmul(left, right):
    return jnp.dot(left, right, preferred_element_type=F32)


def split(value):
    high = value.astype(BF16)
    return high, (value - high.astype(F32)).astype(BF16)


def spread_kernel(tokens_ref, cotangent_ref, out_ref):
    feats = tokens_ref.shape[1]
    for r in range(out_ref.shape[0]):
        out_ref[r, :, :feats] = tokens_ref[...]
        out_ref[r, :, feats:] = cotangent_ref[...]


def own_table_kernel(base_ref, gate_ref, up_ref, down_ref, out_ref):
    del gate_ref, up_ref, down_ref
    for which, sign in ((0, 1.0), (1, -1.0)):
        cos, sin = base_ref[which, 0], base_ref[which, 1]
        span_cos, span_sin = span_table(cos, sin)
        for block in range(out_ref.shape[1] // SPAN):
            at = LOW + MID + block
            c, s = turned(cos[at : at + 1], sin[at : at + 1], span_cos, span_sin)
            rows = slice(block * SPAN, (block + 1) * SPAN)
            out_ref[which, rows, :SPAN] = c.astype(BF16)
            out_ref[which, rows, SPAN:] = (sign * s).astype(BF16)


def project_kernel(x_ref, table_ref, out_ref):
    feats = x_ref.shape[1] // 2
    for which in range(2):
        values = x_ref[:, which * feats : (which + 1) * feats]
        lanes = slice(2 * which * SPAN, 2 * (which + 1) * SPAN)
        out_ref[:, lanes] = matmul(values, table_ref[which]).astype(BF16)


def sum_kernel(*refs):
    total = refs[0][...].astype(F32)
    for ref in refs[1:-1]:
        total += ref[...].astype(F32)
    refs[-1][...] = total.astype(BF16)


def first_kernel(order_ref, x_ref, gate_ref, up_ref, down_ref, *out_refs):
    step = pl.program_id(0)
    wide = gate_ref.shape[1]
    feats = gate_ref.shape[0]
    half = x_ref.shape[0] // 2
    tokens = x_ref[:, :feats]
    cotangent = x_ref[:, feats:]
    parts = (
        matmul(tokens, gate_ref[...]).astype(BF16),
        matmul(tokens, up_ref[...]).astype(BF16),
        against(cotangent, down_ref[...]).astype(BF16),
    )
    for ref, steps, rows in zip(
        out_refs, ((0, 1), (1, 2), (2, 3), (0, 3)), (0, half, 0, half), strict=True
    ):

        @pl.when((step == steps[0]) | (step == steps[1]))
        def _(ref=ref, rows=rows):
            for at, part in enumerate(parts):
                ref[0, :, at * wide : (at + 1) * wide] = part[rows : rows + half]


def fold_kernel(keep_a, keep_b, got_a, got_b, send_a, send_b):
    send_a[...] = (keep_a[0].astype(F32) + got_a[0].astype(F32)).astype(BF16)
    send_b[...] = (keep_b[0].astype(F32) + got_b[0].astype(F32)).astype(BF16)


def close_kernel(keep_a, keep_b, got_a, got_b, last_a, last_b, weight_ref, out_ref):
    del weight_ref
    half = last_a.shape[0]
    out_ref[:half] = (
        keep_a[0].astype(F32) + got_a[0].astype(F32) + last_a[...].astype(F32)
    ).astype(BF16)
    out_ref[half:] = (
        keep_b[0].astype(F32) + got_b[0].astype(F32) + last_b[...].astype(F32)
    ).astype(BF16)


def delta_kernel(
    down_ref, coef_ref, base_ref, turn_ref, base_out_ref, after_ref, out_ref, span, right, table
):
    del after_ref
    step = pl.program_id(0)
    rows, feats = out_ref.shape

    @pl.when(step == 0)
    def _():
        for tile in range(PAD // SPAN):
            lanes = slice(tile * SPAN, (tile + 1) * SPAN)
            sines = slice(PAD + tile * SPAN, PAD + (tile + 1) * SPAN)
            c, s = span_table(base_ref[0, :, lanes], base_ref[1, :, lanes])
            span[0, :, lanes] = c
            span[1, :, lanes] = s
            coef = coef_ref[1:2, lanes] * SCALE_DOWN
            cos, sin = base_out_ref[0, :, lanes], base_out_ref[1, :, lanes]
            span_cos, span_sin = span_table(cos, sin)
            for block in range(feats // SPAN):
                at = LOW + MID + block
                c, s = turned(cos[at : at + 1], sin[at : at + 1], span_cos, span_sin)
                right[block * SPAN : (block + 1) * SPAN, lanes] = (c * coef).astype(BF16)
                right[block * SPAN : (block + 1) * SPAN, sines] = (-s * coef).astype(BF16)

    each = rows // SPAN
    for block in range(each):
        for tile in range(PAD // SPAN):
            lanes = slice(tile * SPAN, (tile + 1) * SPAN)
            cos = turn_ref[0, block : block + 1, lanes]
            sin = turn_ref[0, each + block : each + block + 1, lanes]
            c, s = turned(cos, sin, span[0, :, lanes], span[1, :, lanes])
            units = slice(block * SPAN, (block + 1) * SPAN)
            table[units, lanes] = c.astype(BF16)
            table[units, PAD + tile * SPAN : PAD + (tile + 1) * SPAN] = s.astype(BF16)
    delta = against(table[...], right[...])
    out_ref[...] = (down_ref[...].astype(F32) + delta).astype(BF16)


def summed(ref, first, last):
    total = ref[0, :, first:last].astype(F32)
    for z in range(1, ref.shape[0]):
        total += ref[z, :, first:last].astype(F32)
    return total


def twice(ref, row):
    return jnp.concatenate([ref[row : row + 1], ref[row : row + 1]], axis=1)


def middle_kernel(
    source_ref, sums_ref, proj_ref, coef_ref, base_ref, out_ref, table_ref
):
    wide = table_ref.shape[1]
    for which, sign in ((0, -1.0), (1, 1.0)):
        for tile in range(PAD // SPAN):
            lanes = slice(tile * SPAN, (tile + 1) * SPAN)
            sines = slice(PAD + tile * SPAN, PAD + (tile + 1) * SPAN)
            cos, sin = base_ref[which, 0, :, lanes], base_ref[which, 1, :, lanes]
            span_cos, span_sin = span_table(cos, sin)
            for block in range(wide // SPAN):
                at = LOW + MID + block
                c, s = turned(cos[at : at + 1], sin[at : at + 1], span_cos, span_sin)
                units = slice(block * SPAN, (block + 1) * SPAN)
                table_ref[which, units, lanes] = c.astype(BF16)
                table_ref[which, units, sines] = (sign * s).astype(BF16)

    def kind(k):
        lanes = slice(k * SPAN, (k + 1) * SPAN)
        return [
            proj_ref[source_ref[x], source_ref[4 + c], :, lanes].astype(F32)
            for x in range(proj_ref.shape[0])
            for c in range(proj_ref.shape[1])
        ]

    proj_up = jnp.concatenate(kind(0) + kind(1), axis=1)
    back_down = jnp.concatenate(kind(2) + kind(3), axis=1)
    weighted_up = (proj_up * (twice(coef_ref, 0) * SCALE_UP)).astype(BF16)
    weighted_back = (back_down * (twice(coef_ref, 1) * SCALE_DOWN)).astype(BF16)
    gate = summed(sums_ref, 0, wide)
    up = summed(sums_ref, wide, 2 * wide) + against(weighted_up, table_ref[0])
    dhidden = summed(sums_ref, 2 * wide, 3 * wide) + against(weighted_back, table_ref[1])
    activated = (gate / (1.0 + jnp.exp(-gate))).astype(BF16).astype(F32)
    hidden = (activated * up).astype(BF16)
    dup = (dhidden * activated).astype(BF16)
    back_up = matmul(dup, table_ref[0])
    proj_down = matmul(hidden, table_ref[1])
    up_pairs = jnp.sum(proj_up * back_up, axis=0, keepdims=True)
    down_pairs = jnp.sum(proj_down * back_down, axis=0, keepdims=True)
    grad_up = SCALE_UP * (up_pairs[:, :PAD] + up_pairs[:, PAD:])
    grad_down = SCALE_DOWN * (down_pairs[:, :PAD] + down_pairs[:, PAD:])
    grads = jnp.concatenate(
        [g[:, k * SPAN : (k + 1) * SPAN] for g in (grad_up, grad_down) for k in range(PAD // SPAN)],
        axis=0,
    ).astype(BF16)
    for c in range(out_ref.shape[0]):
        out_ref[c, :, :wide] = hidden
        out_ref[c, :, wide:] = grads


def regroup_kernel(in_ref, out_ref):
    peers, rows, _ = in_ref.shape
    wide = out_ref.shape[1]
    grads = jnp.zeros((rows, SPAN), F32)
    for z in range(peers):
        out_ref[z * rows : (z + 1) * rows, :] = in_ref[z, :, :wide]
        grads += in_ref[z, :, wide:].astype(F32)
    high, low = split(grads)
    out_ref[peers * rows :, :SPAN] = high
    out_ref[peers * rows :, SPAN : 2 * SPAN] = low
    out_ref[peers * rows :, 2 * SPAN :] = jnp.zeros((rows, wide - 2 * SPAN), BF16)


def last_kernel(order_ref, own_ref, one_ref, two_ref, three_ref, weight_ref, out_ref):
    peers, rows, feats = out_ref.shape
    rows //= 2
    wide = own_ref.shape[1]
    count = peers * rows
    total = jnp.zeros((count, feats), F32)
    grads = jnp.zeros((own_ref.shape[0] - count, SPAN), F32)
    for k, ref in enumerate((own_ref, one_ref, two_ref, three_ref)):
        units = pl.ds(pl.multiple_of(order_ref[k] * wide, wide), wide)
        total += matmul(ref[:count, :], weight_ref[units, :])
        grads += ref[count:, :SPAN].astype(F32) + ref[count:, SPAN : 2 * SPAN].astype(F32)
    high, low = split(grads)
    for r in range(peers):
        out_ref[r, :rows, :] = total[r * rows : (r + 1) * rows, :].astype(BF16)
        out_ref[r, rows:, :SPAN] = high
        out_ref[r, rows:, SPAN:] = low


def update_kernel(in_ref, first_ref, second_ref, mixed_ref, step_ref, scratch):
    peers, rows, _ = in_ref.shape
    rows //= 2
    mixed = jnp.zeros(mixed_ref.shape, F32)
    pieces = jnp.zeros((rows, SPAN), F32)
    for r in range(peers):
        mixed += in_ref[r, :rows, :].astype(F32)
        pieces += in_ref[r, rows:, :SPAN].astype(F32)
        pieces += in_ref[r, rows:, SPAN:].astype(F32)
    mixed_ref[...] = mixed.astype(BF16)
    per = PAD // SPAN
    for k in range(rows):
        at = k % per
        scratch[k // per : k // per + 1, at * SPAN : (at + 1) * SPAN] = pieces[k : k + 1]
    grads = scratch[:, :N_COEF]
    squares = jnp.sum(jnp.sum(grads * grads, axis=1, keepdims=True), axis=0, keepdims=True)
    norm_value = jnp.sqrt(squares)
    clipped = grads * jnp.minimum(1.0, 1.0 / (norm_value + 1e-06))
    first = 0.9 * first_ref[...] + 0.1 * clipped
    second = 0.999 * second_ref[...] + 0.001 * clipped * clipped
    step_ref[...] = (
        first / (1.0 - 0.9**ADAM_STEP) / (jnp.sqrt(second / (1.0 - 0.999**ADAM_STEP)) + 1e-08)
    )


def on_device(
    tokens,
    cotangent,
    gate_weight,
    up_weight,
    down_weight,
    coefficients,
    spectral_rows,
    spectral_cols,
    adam_first,
    adam_second,
):
    peers_row = lax.axis_size(PLANE)
    peers_z = lax.axis_size("z")
    peers_y = lax.axis_size("y")
    row_index = lax.axis_index(PLANE)
    z_index = lax.axis_index("z")
    y_index = lax.axis_index("y")
    own, feats = tokens.shape
    units = gate_weight.shape[1]
    wide = units // peers_y
    count = own * peers_row
    feat_first = (z_index * peers_y + y_index) * feats
    unit_first = row_index * units

    def exchange(value, axes):
        return lax.all_to_all(value, axes, 0, 0, tiled=True)

    def padded(values):
        return jnp.pad(values, (0, PAD - N_COEF))

    coefs = jnp.pad(coefficients, ((0, 0), (0, PAD - N_COEF)))
    lanes = row_index * SPAN
    own_left = lax.dynamic_slice_in_dim(padded(spectral_rows[0]), lanes, SPAN)
    own_right = lax.dynamic_slice_in_dim(padded(spectral_cols[1]), lanes, SPAN)
    base_own = jnp.stack(
        [
            phases(own_left, feat_first, feats // SPAN, D),
            phases(own_right, feat_first, feats // SPAN, D),
        ]
    )
    tile_first = unit_first + y_index * wide
    base_tile = jnp.stack(
        [
            phases(padded(spectral_cols[0]), tile_first, wide // SPAN, FF),
            phases(padded(spectral_rows[1]), tile_first, wide // SPAN, FF),
        ]
    )
    base_row = phases(padded(spectral_rows[1]), 0, 0, FF)
    turns = unit_first + SPAN * jnp.arange(units // SPAN, dtype=jnp.int32)
    turns = waves(turns.reshape(-1, 2), padded(spectral_rows[1]), FF, 1)
    turns = turns.reshape(-1, 4, PAD)
    base_out = phases(padded(spectral_cols[1]), feat_first, feats // SPAN, D)

    both = pl.pallas_call(
        spread_kernel,
        in_specs=[VMEM] * 2,
        out_specs=VMEM,
        out_shape=jax.ShapeDtypeStruct((peers_row, own, 2 * feats), BF16),
    )(tokens, cotangent)
    both = exchange(both, PLANE).reshape(count, 2 * feats)

    share = count // peers_z
    half = count // 2
    block = 3 * wide
    order = y_index ^ jnp.array([1, 2, 3, 0], jnp.int32)
    pieces = jax.ShapeDtypeStruct((2, half, block), BF16)

    def piece(at):
        return pl.BlockSpec((1, half, block), lambda i, order: (at(i), 0, 0))

    def full(shape):
        return pl.BlockSpec(shape, lambda i: (0,) * len(shape))

    table = pl.pallas_call(
        own_table_kernel,
        in_specs=[VMEM] * 4,
        out_specs=VMEM,
        out_shape=jax.ShapeDtypeStruct((2, feats, 2 * SPAN), BF16),
        compiler_params=params(8),
    )(base_own, gate_weight, up_weight, down_weight)
    proj = pl.pallas_call(
        project_kernel,
        in_specs=[VMEM] * 2,
        out_specs=VMEM,
        out_shape=jax.ShapeDtypeStruct((count, peers_y * SPAN), BF16),
        compiler_params=params(8),
    )(both, table)
    proj = exchange(proj.reshape(peers_z, share, peers_y * SPAN), "z")
    send_a, send_b, keep_a, keep_b = pl.pallas_call(
        first_kernel,
        grid_spec=pltpu.PrefetchScalarGridSpec(
            num_scalar_prefetch=1,
            grid=(peers_y,),
            in_specs=[
                pl.BlockSpec((count, 2 * feats), lambda i, order: (0, 0)),
                pl.BlockSpec((feats, wide), lambda i, order: (0, order[i])),
                pl.BlockSpec((feats, wide), lambda i, order: (0, order[i])),
                pl.BlockSpec((wide, feats), lambda i, order: (order[i], 0)),
            ],
            out_specs=[
                piece(lambda i: jnp.minimum(i, 1)),
                piece(lambda i: i // 2),
                piece(lambda i: i // 3),
                piece(lambda i: i // 3),
            ],
        ),
        out_shape=[pieces] * 4,
        compiler_params=params(16),
    )(order, both, gate_weight, up_weight, down_weight)

    def swap(value, mask):
        return lax.ppermute(value, "y", [(y, y ^ mask) for y in range(peers_y)])

    got_a, got_b = swap(send_a, 1), swap(send_b, 3)

    def added(values):
        return pl.pallas_call(
            sum_kernel,
            in_specs=[VMEM] * len(values),
            out_specs=VMEM,
            out_shape=jax.ShapeDtypeStruct(values[0].shape, BF16),
            compiler_params=params(8),
        )(*values)

    def turn(value, axis, peers, k):
        return lax.ppermute(value, axis, [(i, (i + k) % peers) for i in range(peers)])

    proj = jnp.sum(proj.astype(F32), axis=0).astype(BF16)
    proj = added([proj] + [turn(proj, "y", peers_y, k) for k in (1, 2, 3)])
    proj = jnp.stack([proj, lax.ppermute(proj, "core", [(0, 1), (1, 0)])])
    proj = jnp.stack([proj] + [turn(proj, "x", 4, k) for k in (1, 2, 3)])
    chip = (lax.axis_index("x") - jnp.arange(4, dtype=jnp.int32)) & 3
    core = lax.axis_index("core") ^ jnp.arange(2, dtype=jnp.int32)
    source = jnp.concatenate([chip, core])

    def whole(rows):
        return pl.BlockSpec((1, half, block), lambda i: (rows, 0, 0))

    send_a, send_b = pl.pallas_call(
        fold_kernel,
        grid=(1,),
        in_specs=[whole(0), whole(0), whole(1), whole(0)],
        out_specs=[full((half, block))] * 2,
        out_shape=[jax.ShapeDtypeStruct((half, block), BF16)] * 2,
        compiler_params=params(12),
    )(keep_a, keep_b, got_a, got_b)
    last_a, last_b = swap(send_a, 3), swap(send_b, 1)
    blocks = 14
    weight = pl.pallas_call(
        delta_kernel,
        grid=(blocks,),
        in_specs=[
            pl.BlockSpec((units // blocks, feats), lambda i: (i, 0)),
            pl.BlockSpec(coefs.shape, lambda i: (0, 0)),
            pl.BlockSpec(base_row.shape, lambda i: (0, 0, 0)),
            pl.BlockSpec((1,) + turns.shape[1:], lambda i: (i, 0, 0)),
            pl.BlockSpec(base_out.shape, lambda i: (0, 0, 0)),
            pl.BlockSpec(memory_space=pl.ANY),
        ],
        out_specs=pl.BlockSpec((units // blocks, feats), lambda i: (i, 0)),
        out_shape=jax.ShapeDtypeStruct((units, feats), BF16),
        scratch_shapes=[
            pltpu.VMEM((2, SPAN, PAD), F32),
            pltpu.VMEM((feats, 2 * PAD), BF16),
            pltpu.VMEM((units // blocks, 2 * PAD), BF16),
        ],
        compiler_params=params(12),
        cost_estimate=pl.CostEstimate(flops=8 << 30, bytes_accessed=32 << 20, transcendentals=0),
    )(down_weight, coefs, base_row, turns, base_out, send_a)

    sums = pl.pallas_call(
        close_kernel,
        grid=(1,),
        in_specs=[whole(1), whole(1), whole(0), whole(1)] + [full((half, block))] * 2
        + [pl.BlockSpec(memory_space=pl.ANY)],
        out_specs=full((count, block)),
        out_shape=jax.ShapeDtypeStruct((count, block), BF16),
        compiler_params=params(12),
    )(keep_a, keep_b, got_a, got_b, last_a, last_b, weight)
    sums = exchange(sums.reshape(peers_z, share, block), "z")

    hidden = pl.pallas_call(
        middle_kernel,
        in_specs=[pl.BlockSpec(memory_space=pltpu.SMEM)] + [VMEM] * 4,
        out_specs=VMEM,
        out_shape=jax.ShapeDtypeStruct((peers_z, share, wide + SPAN), BF16),
        scratch_shapes=[pltpu.VMEM((2, wide, 2 * PAD), BF16)],
        compiler_params=params(20),
    )(source, sums, proj, coefs, base_tile)
    hidden = exchange(hidden, "z")
    hidden = pl.pallas_call(
        regroup_kernel,
        in_specs=[VMEM],
        out_specs=VMEM,
        out_shape=jax.ShapeDtypeStruct((count + share, wide), BF16),
        compiler_params=params(8),
    )(hidden)

    def shifted(k):
        return lax.ppermute(hidden, "y", [(y, (y + k) % peers_y) for y in range(peers_y)])

    others = [shifted(1), shifted(2), shifted(3)]
    sources = (y_index - jnp.arange(peers_y, dtype=jnp.int32)) & 3
    mixed = pl.pallas_call(
        last_kernel,
        in_specs=[pl.BlockSpec(memory_space=pltpu.SMEM)] + [VMEM] * 5,
        out_specs=VMEM,
        out_shape=jax.ShapeDtypeStruct((peers_row, 2 * own, feats), BF16),
        compiler_params=params(12),
    )(sources, hidden, *others, weight)
    mixed = exchange(mixed, PLANE)

    return pl.pallas_call(
        update_kernel,
        in_specs=[VMEM] * 3,
        out_specs=[VMEM] * 2,
        out_shape=[
            jax.ShapeDtypeStruct((own, feats), BF16),
            jax.ShapeDtypeStruct(adam_first.shape, F32),
        ],
        scratch_shapes=[pltpu.VMEM((2, PAD), F32)],
    )(mixed, adam_first, adam_second)


def solution(mesh):
    chips = Mesh(mesh.devices.reshape(4, 2, 8, 4), ("x", "core", "z", "y"))
    tiles = P(("x", "core"), ("z", "y"))
    weights = P(("z", "y"), ("x", "core"))
    placed = (tiles, tiles, weights, weights, tiles, P(), P(), P(), P(), P())
    return jax.shard_map(
        on_device, mesh=chips, in_specs=placed, out_specs=(tiles, P()), check_vma=False
    )
```

```python
import math

import jax
import jax.numpy as jnp
from jax import lax
from jax.experimental import pallas as pl
from jax.experimental.pallas import tpu as pltpu
from jax.sharding import Mesh
from jax.sharding import PartitionSpec as P

D = 8192
FF = 28672
N_COEF = 1000
ADAM_STEP = 3
PAD = 1024
SCALE_UP = 1.0 / math.sqrt(2.0 * D * N_COEF)
SCALE_DOWN = 1.0 / math.sqrt(2.0 * FF * N_COEF)
TWO_PI = 6.283185307179586

F32 = jnp.float32
BF16 = jnp.bfloat16
LOW = 8
MID = 16
SPAN = LOW * MID

PLANE = ("x", "core")
VMEM = pl.BlockSpec(memory_space=pltpu.VMEM)


def params(mib):
    return pltpu.CompilerParams(vmem_limit_bytes=mib << 20)


def waves(index, freq, width, axis):
    phase = index[..., None] * freq % width
    angle = phase.astype(F32) * (TWO_PI / width)
    return jnp.stack([jnp.cos(angle), jnp.sin(angle)], axis=axis)


def phases(freq, first, blocks, width):
    rows = -(-(LOW + MID + blocks) // 8) * 8
    index = jnp.concatenate(
        [
            jnp.arange(LOW, dtype=jnp.int32),
            LOW * jnp.arange(MID, dtype=jnp.int32),
            first + SPAN * jnp.arange(blocks, dtype=jnp.int32),
            jnp.zeros(rows - LOW - MID - blocks, jnp.int32),
        ]
    )
    return waves(index, freq, width, 0)


def span_table(cos, sin):
    low_cos, low_sin = cos[:LOW], sin[:LOW]
    out_cos, out_sin = [], []
    for k in range(MID):
        a, b = cos[LOW + k : LOW + k + 1], sin[LOW + k : LOW + k + 1]
        out_cos.append(a * low_cos - b * low_sin)
        out_sin.append(b * low_cos + a * low_sin)
    return jnp.concatenate(out_cos, axis=0), jnp.concatenate(out_sin, axis=0)


def turned(cos, sin, span_cos, span_sin):
    return cos * span_cos - sin * span_sin, sin * span_cos + cos * span_sin


def against(left, table):
    return lax.dot_general(
        left, table, (((1,), (1,)), ((), ())), preferred_element_type=F32
    )


def matmul(left, right):
    return jnp.dot(left, right, preferred_element_type=F32)


def split(value):
    high = value.astype(BF16)
    return high, (value - high.astype(F32)).astype(BF16)


def spread_kernel(tokens_ref, cotangent_ref, out_ref):
    feats = tokens_ref.shape[1]
    for r in range(out_ref.shape[0]):
        out_ref[r, :, :feats] = tokens_ref[...]
        out_ref[r, :, feats:] = cotangent_ref[...]


def own_table_kernel(base_ref, out_ref):
    for which, sign in ((0, 1.0), (1, -1.0)):
        cos, sin = base_ref[which, 0], base_ref[which, 1]
        span_cos, span_sin = span_table(cos, sin)
        for block in range(out_ref.shape[1] // SPAN):
            at = LOW + MID + block
            c, s = turned(cos[at : at + 1], sin[at : at + 1], span_cos, span_sin)
            rows = slice(block * SPAN, (block + 1) * SPAN)
            out_ref[which, rows, :SPAN] = c.astype(BF16)
            out_ref[which, rows, SPAN:] = (sign * s).astype(BF16)


def late_kernel(rows_ref, cols_ref, coef_ref, after_ref, freq_ref, coef_out):
    del after_ref
    freq_ref[...] = jnp.zeros(freq_ref.shape, jnp.int32)
    coef_out[...] = jnp.zeros(coef_out.shape, F32)
    freq_ref[0:2, :N_COEF] = rows_ref[...]
    freq_ref[2:4, :N_COEF] = cols_ref[...]
    coef_out[:, :N_COEF] = coef_ref[...]


def sum_kernel(*refs):
    total = refs[0][...].astype(F32)
    for ref in refs[1:-1]:
        total += ref[...].astype(F32)
    refs[-1][...] = total.astype(BF16)


def project_kernel(x_ref, table_ref, after_ref, out_ref):
    del after_ref
    feats = x_ref.shape[1] // 2
    for which in range(2):
        values = x_ref[:, which * feats : (which + 1) * feats]
        lanes = slice(2 * which * SPAN, 2 * (which + 1) * SPAN)
        out_ref[:, lanes] = matmul(values, table_ref[which]).astype(BF16)


def first_kernel(
    order_ref, x_ref, gate_ref, up_ref, down_ref, *refs
):
    out_refs, (gates, ups, downs, sems) = refs[:4], refs[4:]
    _, feats, wide = gates.shape
    half = x_ref.shape[0] // 2
    copies = []
    for i in range(gates.shape[0]):
        units = pl.ds(pl.multiple_of(order_ref[i] * wide, SPAN), wide)
        copies.append(
            (
                pltpu.make_async_copy(gate_ref.at[:, units], gates.at[i], sems.at[i, 0]),
                pltpu.make_async_copy(up_ref.at[:, units], ups.at[i], sems.at[i, 1]),
                pltpu.make_async_copy(down_ref.at[units, :], downs.at[i], sems.at[i, 2]),
            )
        )
        for copy in copies[-1]:
            copy.start()
    tokens = x_ref[:, :feats]
    cotangent = x_ref[:, feats:]
    send_a, send_b, keep_a, keep_b = out_refs
    places = (
        ((send_a, 0), (keep_b, 0)),
        ((send_a, 1), (send_b, 0)),
        ((keep_a, 0), (send_b, 1)),
        ((keep_a, 1), (keep_b, 1)),
    )
    for i, (low, high) in enumerate(places):
        for copy in copies[i]:
            copy.wait()
        parts = (
            matmul(tokens, gates[i]),
            matmul(tokens, ups[i]),
            against(cotangent, downs[i]),
        )
        for at, part in enumerate(parts):
            lanes = slice(at * wide, (at + 1) * wide)
            low[0][low[1], :, lanes] = part[:half].astype(BF16)
            high[0][high[1], :, lanes] = part[half:].astype(BF16)


def fold_kernel(keep_a, keep_b, got_a, got_b, send_a, send_b):
    send_a[...] = (keep_a[0].astype(F32) + got_a[0].astype(F32)).astype(BF16)
    send_b[...] = (keep_b[0].astype(F32) + got_b[0].astype(F32)).astype(BF16)


def close_kernel(keep_a, keep_b, got_a, got_b, last_a, last_b, proj_ref, out_ref, proj_out):
    proj_out[...] = proj_ref[...]
    half = last_a.shape[0]
    out_ref[:half] = (
        keep_a[0].astype(F32) + got_a[0].astype(F32) + last_a[...].astype(F32)
    ).astype(BF16)
    out_ref[half:] = (
        keep_b[0].astype(F32) + got_b[0].astype(F32) + last_b[...].astype(F32)
    ).astype(BF16)


def delta_kernel(
    order_ref, down_ref, coef_ref, base_ref, base_out_ref, turn_ref, after_ref, out_ref, *scratch
):
    del after_ref
    left, right, right_turned, down, sems = scratch
    step = pl.program_id(0)
    wide, feats = out_ref.shape
    count = order_ref.shape[0]

    def copy(k):
        units = pl.ds(pl.multiple_of(order_ref[k] * wide, SPAN), wide)
        return pltpu.make_async_copy(down_ref.at[units], down.at[k], sems.at[k])

    @pl.when(step == 0)
    def _():
        for k in range(count):
            copy(k).start()
        for tile in range(PAD // SPAN):
            lanes = slice(tile * SPAN, (tile + 1) * SPAN)
            sines = slice(PAD + tile * SPAN, PAD + (tile + 1) * SPAN)
            cos, sin = base_ref[0, :, lanes], base_ref[1, :, lanes]
            span_cos, span_sin = span_table(cos, sin)
            for block in range(wide // SPAN):
                at = LOW + MID + block
                c, s = turned(cos[at : at + 1], sin[at : at + 1], span_cos, span_sin)
                units = slice(block * SPAN, (block + 1) * SPAN)
                left[units, lanes] = c.astype(BF16)
                left[units, sines] = s.astype(BF16)
            coef = coef_ref[1:2, lanes] * SCALE_DOWN
            cos, sin = base_out_ref[0, :, lanes], base_out_ref[1, :, lanes]
            span_cos, span_sin = span_table(cos, sin)
            for block in range(feats // SPAN):
                at = LOW + MID + block
                c, s = turned(cos[at : at + 1], sin[at : at + 1], span_cos, span_sin)
                rows = slice(block * SPAN, (block + 1) * SPAN)
                right[0, rows, lanes] = c * coef
                right[1, rows, lanes] = -s * coef

    for tile in range(PAD // SPAN):
        lanes = slice(tile * SPAN, (tile + 1) * SPAN)
        sines = slice(PAD + tile * SPAN, PAD + (tile + 1) * SPAN)
        cos, sin = turn_ref[0, 0:1, lanes], turn_ref[0, 1:2, lanes]
        for rows in (slice(i, i + 64) for i in range(0, feats, 64)):
            c, s = right[0, rows, lanes], right[1, rows, lanes]
            right_turned[rows, lanes] = (cos * c + sin * s).astype(BF16)
            right_turned[rows, sines] = (cos * s - sin * c).astype(BF16)
    delta = against(left[...], right_turned[...])
    copy(step).wait()
    out_ref[...] = (down[step].astype(F32) + delta).astype(BF16)


def summed(ref, first, last):
    total = ref[0, :, first:last].astype(F32)
    for z in range(1, ref.shape[0]):
        total += ref[z, :, first:last].astype(F32)
    return total


def twice(ref, row):
    return jnp.concatenate([ref[row : row + 1], ref[row : row + 1]], axis=1)


def middle_kernel(
    source_ref, sums_ref, proj_ref, coef_ref, base_ref, out_ref, table_ref
):
    wide = table_ref.shape[1]
    for which, sign in ((0, -1.0), (1, 1.0)):
        for tile in range(PAD // SPAN):
            lanes = slice(tile * SPAN, (tile + 1) * SPAN)
            sines = slice(PAD + tile * SPAN, PAD + (tile + 1) * SPAN)
            cos, sin = base_ref[which, 0, :, lanes], base_ref[which, 1, :, lanes]
            span_cos, span_sin = span_table(cos, sin)
            for block in range(wide // SPAN):
                at = LOW + MID + block
                c, s = turned(cos[at : at + 1], sin[at : at + 1], span_cos, span_sin)
                units = slice(block * SPAN, (block + 1) * SPAN)
                table_ref[which, units, lanes] = c.astype(BF16)
                table_ref[which, units, sines] = (sign * s).astype(BF16)

    def kind(k):
        lanes = slice(k * SPAN, (k + 1) * SPAN)
        return [
            proj_ref[source_ref[x], source_ref[4 + c], :, lanes].astype(F32)
            for x in range(proj_ref.shape[0])
            for c in range(proj_ref.shape[1])
        ]

    proj_up = jnp.concatenate(kind(0) + kind(1), axis=1)
    back_down = jnp.concatenate(kind(2) + kind(3), axis=1)
    weighted_up = (proj_up * (twice(coef_ref, 0) * SCALE_UP)).astype(BF16)
    weighted_back = (back_down * (twice(coef_ref, 1) * SCALE_DOWN)).astype(BF16)
    gate = summed(sums_ref, 0, wide)
    up = summed(sums_ref, wide, 2 * wide) + against(weighted_up, table_ref[0])
    dhidden = summed(sums_ref, 2 * wide, 3 * wide) + against(weighted_back, table_ref[1])
    activated = (gate / (1.0 + jnp.exp(-gate))).astype(BF16).astype(F32)
    hidden = (activated * up).astype(BF16)
    dup = (dhidden * activated).astype(BF16)
    back_up = matmul(dup, table_ref[0])
    proj_down = matmul(hidden, table_ref[1])
    up_pairs = jnp.sum(proj_up * back_up, axis=0, keepdims=True)
    down_pairs = jnp.sum(proj_down * back_down, axis=0, keepdims=True)
    grad_up = SCALE_UP * (up_pairs[:, :PAD] + up_pairs[:, PAD:])
    grad_down = SCALE_DOWN * (down_pairs[:, :PAD] + down_pairs[:, PAD:])
    grads = jnp.concatenate(
        [g[:, k * SPAN : (k + 1) * SPAN] for g in (grad_up, grad_down) for k in range(PAD // SPAN)],
        axis=0,
    ).astype(BF16)
    for c in range(out_ref.shape[0]):
        out_ref[c, :, :wide] = hidden
        out_ref[c, :, wide:] = grads


def regroup_kernel(in_ref, out_ref):
    peers, rows, _ = in_ref.shape
    wide = out_ref.shape[1]
    grads = jnp.zeros((rows, SPAN), F32)
    for z in range(peers):
        out_ref[z * rows : (z + 1) * rows, :] = in_ref[z, :, :wide]
        grads += in_ref[z, :, wide:].astype(F32)
    high, low = split(grads)
    out_ref[peers * rows :, :SPAN] = high
    out_ref[peers * rows :, SPAN : 2 * SPAN] = low
    out_ref[peers * rows :, 2 * SPAN :] = jnp.zeros((rows, wide - 2 * SPAN), BF16)


def last_kernel(own_ref, one_ref, two_ref, three_ref, weight_ref, out_ref):
    peers, rows, feats = out_ref.shape
    rows //= 2
    wide = own_ref.shape[1]
    count = peers * rows
    total = jnp.zeros((count, feats), F32)
    grads = jnp.zeros((own_ref.shape[0] - count, SPAN), F32)
    for k, ref in enumerate((own_ref, one_ref, two_ref, three_ref)):
        units = slice(k * wide, (k + 1) * wide)
        total += matmul(ref[:count, :], weight_ref[units, :])
        grads += ref[count:, :SPAN].astype(F32) + ref[count:, SPAN : 2 * SPAN].astype(F32)
    high, low = split(grads)
    for r in range(peers):
        out_ref[r, :rows, :] = total[r * rows : (r + 1) * rows, :].astype(BF16)
        out_ref[r, rows:, :SPAN] = high
        out_ref[r, rows:, SPAN:] = low


def update_kernel(in_ref, first_ref, second_ref, mixed_ref, step_ref, scratch):
    peers, rows, _ = in_ref.shape
    rows //= 2
    mixed = jnp.zeros(mixed_ref.shape, F32)
    pieces = jnp.zeros((rows, SPAN), F32)
    for r in range(peers):
        mixed += in_ref[r, :rows, :].astype(F32)
        pieces += in_ref[r, rows:, :SPAN].astype(F32)
        pieces += in_ref[r, rows:, SPAN:].astype(F32)
    mixed_ref[...] = mixed.astype(BF16)
    per = PAD // SPAN
    for k in range(rows):
        at = k % per
        scratch[k // per : k // per + 1, at * SPAN : (at + 1) * SPAN] = pieces[k : k + 1]
    grads = scratch[:, :N_COEF]
    squares = jnp.sum(jnp.sum(grads * grads, axis=1, keepdims=True), axis=0, keepdims=True)
    norm_value = jnp.sqrt(squares)
    clipped = grads * jnp.minimum(1.0, 1.0 / (norm_value + 1e-06))
    first = 0.9 * first_ref[...] + 0.1 * clipped
    second = 0.999 * second_ref[...] + 0.001 * clipped * clipped
    step_ref[...] = (
        first / (1.0 - 0.9**ADAM_STEP) / (jnp.sqrt(second / (1.0 - 0.999**ADAM_STEP)) + 1e-08)
    )


def on_device(
    tokens,
    cotangent,
    gate_weight,
    up_weight,
    down_weight,
    coefficients,
    spectral_rows,
    spectral_cols,
    adam_first,
    adam_second,
):
    peers_row = lax.axis_size(PLANE)
    peers_z = lax.axis_size("z")
    peers_y = lax.axis_size("y")
    row_index = lax.axis_index(PLANE)
    z_index = lax.axis_index("z")
    y_index = lax.axis_index("y")
    own, feats = tokens.shape
    units = gate_weight.shape[1]
    wide = units // peers_y
    count = own * peers_row
    feat_first = (z_index * peers_y + y_index) * feats
    unit_first = row_index * units

    def exchange(value, axes):
        return lax.all_to_all(value, axes, 0, 0, tiled=True)

    def padded(values):
        return jnp.pad(values, (0, PAD - N_COEF))

    lanes = row_index * SPAN
    own_left = lax.dynamic_slice_in_dim(padded(spectral_rows[0]), lanes, SPAN)
    own_right = lax.dynamic_slice_in_dim(padded(spectral_cols[1]), lanes, SPAN)
    base_own = jnp.stack(
        [
            phases(own_left, feat_first, feats // SPAN, D),
            phases(own_right, feat_first, feats // SPAN, D),
        ]
    )

    both = pl.pallas_call(
        spread_kernel,
        in_specs=[VMEM] * 2,
        out_specs=VMEM,
        out_shape=jax.ShapeDtypeStruct((peers_row, own, 2 * feats), BF16),
    )(tokens, cotangent)
    both = exchange(both, PLANE).reshape(count, 2 * feats)

    share = count // peers_z
    half = count // 2
    block = 3 * wide
    smem = pl.BlockSpec(memory_space=pltpu.SMEM)
    hbm = pl.BlockSpec(memory_space=pltpu.HBM)
    anywhere = pl.BlockSpec(memory_space=pl.ANY)
    order = y_index ^ jnp.array([1, 2, 3, 0], jnp.int32)
    pieces = jax.ShapeDtypeStruct((2, half, block), BF16)

    def full(shape):
        return pl.BlockSpec(shape, lambda i: (0,) * len(shape))

    table = pl.pallas_call(
        own_table_kernel,
        in_specs=[VMEM],
        out_specs=VMEM,
        out_shape=jax.ShapeDtypeStruct((2, feats, 2 * SPAN), BF16),
        compiler_params=params(8),
    )(base_own)
    send_a, send_b, keep_a, keep_b = pl.pallas_call(
        first_kernel,
        in_specs=[smem, VMEM, hbm, hbm, hbm],
        out_specs=[VMEM] * 4,
        out_shape=[pieces] * 4,
        scratch_shapes=[
            pltpu.VMEM((peers_y, feats, wide), BF16),
            pltpu.VMEM((peers_y, feats, wide), BF16),
            pltpu.VMEM((peers_y, wide, feats), BF16),
            pltpu.SemaphoreType.DMA((peers_y, 3)),
        ],
        compiler_params=params(60),
    )(order, both, gate_weight, up_weight, down_weight)

    def swap(value, mask):
        return lax.ppermute(value, "y", [(y, y ^ mask) for y in range(peers_y)])

    got_a, got_b = swap(send_a, 1), swap(send_b, 3)
    proj = pl.pallas_call(
        project_kernel,
        in_specs=[VMEM] * 2 + [anywhere],
        out_specs=VMEM,
        out_shape=jax.ShapeDtypeStruct((count, peers_y * SPAN), BF16),
        compiler_params=params(8),
    )(both, table, keep_a)
    proj = exchange(proj.reshape(peers_z, share, peers_y * SPAN), "z")

    freq, coefs = pl.pallas_call(
        late_kernel,
        in_specs=[VMEM] * 3 + [anywhere],
        out_specs=[VMEM] * 2,
        out_shape=[
            jax.ShapeDtypeStruct((4, PAD), jnp.int32),
            jax.ShapeDtypeStruct((2, PAD), F32),
        ],
    )(spectral_rows, spectral_cols, coefficients, keep_a)
    tile_first = unit_first + y_index * wide
    base_up = phases(freq[2], tile_first, wide // SPAN, FF)
    base_down = phases(freq[1], tile_first, wide // SPAN, FF)
    base_out = phases(freq[3], feat_first, feats // SPAN, D)
    sources = (y_index - jnp.arange(peers_y, dtype=jnp.int32)) & 3
    turns = waves(((sources - y_index) * wide)[:, None], freq[1], FF, 1)
    turns = turns.reshape(peers_y, 2, PAD)

    def added(values):
        return pl.pallas_call(
            sum_kernel,
            in_specs=[VMEM] * len(values),
            out_specs=VMEM,
            out_shape=jax.ShapeDtypeStruct(values[0].shape, BF16),
            compiler_params=params(8),
        )(*values)

    def turn(value, axis, peers, k):
        return lax.ppermute(value, axis, [(i, (i + k) % peers) for i in range(peers)])

    proj = jnp.sum(proj.astype(F32), axis=0).astype(BF16)
    proj = added([proj] + [turn(proj, "y", peers_y, k) for k in (1, 2, 3)])
    def whole(rows):
        return pl.BlockSpec((1, half, block), lambda i: (rows, 0, 0))

    send_a, send_b = pl.pallas_call(
        fold_kernel,
        grid=(1,),
        in_specs=[whole(0), whole(0), whole(1), whole(0)],
        out_specs=[full((half, block))] * 2,
        out_shape=[jax.ShapeDtypeStruct((half, block), BF16)] * 2,
        compiler_params=params(12),
    )(keep_a, keep_b, got_a, got_b)
    last_a, last_b = swap(send_a, 3), swap(send_b, 1)
    sums, proj = pl.pallas_call(
        close_kernel,
        grid=(1,),
        in_specs=[whole(1), whole(1), whole(0), whole(1)] + [full((half, block))] * 2
        + [full(proj.shape)],
        out_specs=[full((count, block)), full(proj.shape)],
        out_shape=[
            jax.ShapeDtypeStruct((count, block), BF16),
            jax.ShapeDtypeStruct(proj.shape, BF16),
        ],
        compiler_params=params(12),
    )(keep_a, keep_b, got_a, got_b, last_a, last_b, proj)
    proj = jnp.stack([proj, lax.ppermute(proj, "core", [(0, 1), (1, 0)])])
    proj = jnp.stack([proj] + [turn(proj, "x", 4, k) for k in (1, 2, 3)])
    chip = (lax.axis_index("x") - jnp.arange(4, dtype=jnp.int32)) & 3
    core = lax.axis_index("core") ^ jnp.arange(2, dtype=jnp.int32)
    source = jnp.concatenate([chip, core])
    sums = exchange(sums.reshape(peers_z, share, block), "z")

    hidden = pl.pallas_call(
        middle_kernel,
        in_specs=[smem] + [VMEM] * 4,
        out_specs=VMEM,
        out_shape=jax.ShapeDtypeStruct((peers_z, share, wide + SPAN), BF16),
        scratch_shapes=[pltpu.VMEM((2, wide, 2 * PAD), BF16)],
        compiler_params=params(20),
    )(source, sums, proj, coefs, jnp.stack([base_up, base_down]))
    hidden = exchange(hidden, "z")
    hidden = pl.pallas_call(
        regroup_kernel,
        in_specs=[VMEM],
        out_specs=VMEM,
        out_shape=jax.ShapeDtypeStruct((count + share, wide), BF16),
        compiler_params=params(8),
    )(hidden)
    weight = pl.pallas_call(
        delta_kernel,
        grid=(peers_y,),
        in_specs=[
            smem,
            hbm,
            full(coefs.shape),
            full(base_down.shape),
            full(base_out.shape),
            pl.BlockSpec((1,) + turns.shape[1:], lambda i: (i, 0, 0)),
            anywhere,
        ],
        out_specs=pl.BlockSpec((wide, feats), lambda i: (i, 0)),
        out_shape=jax.ShapeDtypeStruct((units, feats), BF16),
        scratch_shapes=[
            pltpu.VMEM((wide, 2 * PAD), BF16),
            pltpu.VMEM((2, feats, PAD), F32),
            pltpu.VMEM((feats, 2 * PAD), BF16),
            pltpu.VMEM((peers_y, wide, feats), BF16),
            pltpu.SemaphoreType.DMA((peers_y,)),
        ],
        compiler_params=params(20),
        cost_estimate=pl.CostEstimate(
            flops=6 << 30, bytes_accessed=8 << 20, transcendentals=0
        ),
    )(sources, down_weight, coefs, base_down, base_out, turns, hidden)

    def shifted(k):
        return lax.ppermute(hidden, "y", [(y, (y + k) % peers_y) for y in range(peers_y)])

    others = [shifted(1), shifted(2), shifted(3)]
    mixed = pl.pallas_call(
        last_kernel,
        in_specs=[VMEM] * 5,
        out_specs=VMEM,
        out_shape=jax.ShapeDtypeStruct((peers_row, 2 * own, feats), BF16),
        compiler_params=params(12),
    )(hidden, *others, weight)
    mixed = exchange(mixed, PLANE)

    return pl.pallas_call(
        update_kernel,
        in_specs=[VMEM] * 3,
        out_specs=[VMEM] * 2,
        out_shape=[
            jax.ShapeDtypeStruct((own, feats), BF16),
            jax.ShapeDtypeStruct(adam_first.shape, F32),
        ],
        scratch_shapes=[pltpu.VMEM((2, PAD), F32)],
    )(mixed, adam_first, adam_second)


def solution(mesh):
    chips = Mesh(mesh.devices.reshape(4, 2, 8, 4), ("x", "core", "z", "y"))
    tiles = P(("x", "core"), ("z", "y"))
    weights = P(("z", "y"), ("x", "core"))
    placed = (tiles, tiles, weights, weights, tiles, P(), P(), P(), P(), P())
    return jax.shard_map(
        on_device, mesh=chips, in_specs=placed, out_specs=(tiles, P()), check_vma=False
    )
```

```python
import math

import jax
import jax.numpy as jnp
from jax import lax
from jax.experimental import pallas as pl
from jax.experimental.pallas import tpu as pltpu
from jax.sharding import Mesh
from jax.sharding import PartitionSpec as P

D = 8192
FF = 28672
N_COEF = 1000
ADAM_STEP = 3
PAD = 1024
SCALE_UP = 1.0 / math.sqrt(2.0 * D * N_COEF)
SCALE_DOWN = 1.0 / math.sqrt(2.0 * FF * N_COEF)
TWO_PI = 6.283185307179586

F32 = jnp.float32
BF16 = jnp.bfloat16
LOW = 8
MID = 16
SPAN = LOW * MID

PLANE = ("x", "core")
VMEM = pl.BlockSpec(memory_space=pltpu.VMEM)


def params(mib):
    return pltpu.CompilerParams(vmem_limit_bytes=mib << 20)


def waves(index, freq, width, axis):
    phase = index[..., None] * freq % width
    angle = phase.astype(F32) * (TWO_PI / width)
    return jnp.stack([jnp.cos(angle), jnp.sin(angle)], axis=axis)


def phases(freq, first, blocks, width):
    rows = -(-(LOW + MID + blocks) // 8) * 8
    index = jnp.concatenate(
        [
            jnp.arange(LOW, dtype=jnp.int32),
            LOW * jnp.arange(MID, dtype=jnp.int32),
            first + SPAN * jnp.arange(blocks, dtype=jnp.int32),
            jnp.zeros(rows - LOW - MID - blocks, jnp.int32),
        ]
    )
    return waves(index, freq, width, 0)


def span_table(cos, sin):
    low_cos, low_sin = cos[:LOW], sin[:LOW]
    out_cos, out_sin = [], []
    for k in range(MID):
        a, b = cos[LOW + k : LOW + k + 1], sin[LOW + k : LOW + k + 1]
        out_cos.append(a * low_cos - b * low_sin)
        out_sin.append(b * low_cos + a * low_sin)
    return jnp.concatenate(out_cos, axis=0), jnp.concatenate(out_sin, axis=0)


def turned(cos, sin, span_cos, span_sin):
    return cos * span_cos - sin * span_sin, sin * span_cos + cos * span_sin


def against(left, table):
    return lax.dot_general(
        left, table, (((1,), (1,)), ((), ())), preferred_element_type=F32
    )


def matmul(left, right):
    return jnp.dot(left, right, preferred_element_type=F32)


def split(value):
    high = value.astype(BF16)
    return high, (value - high.astype(F32)).astype(BF16)


def spread_kernel(tokens_ref, cotangent_ref, out_ref):
    feats = tokens_ref.shape[1]
    for r in range(out_ref.shape[0]):
        out_ref[r, :, :feats] = tokens_ref[...]
        out_ref[r, :, feats:] = cotangent_ref[...]


def own_table_kernel(base_ref, out_ref):
    for which, sign in ((0, 1.0), (1, -1.0)):
        cos, sin = base_ref[which, 0], base_ref[which, 1]
        span_cos, span_sin = span_table(cos, sin)
        for block in range(out_ref.shape[1] // SPAN):
            at = LOW + MID + block
            c, s = turned(cos[at : at + 1], sin[at : at + 1], span_cos, span_sin)
            rows = slice(block * SPAN, (block + 1) * SPAN)
            out_ref[which, rows, :SPAN] = c.astype(BF16)
            out_ref[which, rows, SPAN:] = (sign * s).astype(BF16)


def late_kernel(rows_ref, cols_ref, coef_ref, after_ref, freq_ref, coef_out):
    del after_ref
    freq_ref[...] = jnp.zeros(freq_ref.shape, jnp.int32)
    coef_out[...] = jnp.zeros(coef_out.shape, F32)
    freq_ref[0:2, :N_COEF] = rows_ref[...]
    freq_ref[2:4, :N_COEF] = cols_ref[...]
    coef_out[:, :N_COEF] = coef_ref[...]


def sum_kernel(*refs):
    total = refs[0][...].astype(F32)
    for ref in refs[1:-1]:
        total += ref[...].astype(F32)
    refs[-1][...] = total.astype(BF16)


def project_kernel(x_ref, table_ref, after_ref, out_ref):
    del after_ref
    feats = x_ref.shape[1] // 2
    for which in range(2):
        values = x_ref[:, which * feats : (which + 1) * feats]
        lanes = slice(2 * which * SPAN, 2 * (which + 1) * SPAN)
        out_ref[:, lanes] = matmul(values, table_ref[which]).astype(BF16)


def first_kernel(
    order_ref, x_ref, gate_ref, up_ref, down_ref, *refs
):
    out_refs, (gates, ups, downs, sems) = refs[:4], refs[4:]
    _, feats, wide = gates.shape
    half = x_ref.shape[0] // 2
    copies = []
    for i in range(gates.shape[0]):
        units = pl.ds(pl.multiple_of(order_ref[i] * wide, SPAN), wide)
        copies.append(
            (
                pltpu.make_async_copy(gate_ref.at[:, units], gates.at[i], sems.at[i, 0]),
                pltpu.make_async_copy(up_ref.at[:, units], ups.at[i], sems.at[i, 1]),
                pltpu.make_async_copy(down_ref.at[units, :], downs.at[i], sems.at[i, 2]),
            )
        )
        for copy in copies[-1]:
            copy.start()
    tokens = x_ref[:, :feats]
    cotangent = x_ref[:, feats:]
    send_a, send_b, keep_a, keep_b = out_refs
    places = (
        ((send_a, 0), (keep_b, 0)),
        ((send_a, 1), (send_b, 0)),
        ((keep_a, 0), (send_b, 1)),
        ((keep_a, 1), (keep_b, 1)),
    )
    for i, (low, high) in enumerate(places):
        for copy in copies[i]:
            copy.wait()
        parts = (
            matmul(tokens, gates[i]),
            matmul(tokens, ups[i]),
            against(cotangent, downs[i]),
        )
        for at, part in enumerate(parts):
            lanes = slice(at * wide, (at + 1) * wide)
            low[0][low[1], :, lanes] = part[:half].astype(BF16)
            high[0][high[1], :, lanes] = part[half:].astype(BF16)


def fold_kernel(keep_a, keep_b, got_a, got_b, send_a, send_b):
    send_a[...] = (keep_a[0].astype(F32) + got_a[0].astype(F32)).astype(BF16)
    send_b[...] = (keep_b[0].astype(F32) + got_b[0].astype(F32)).astype(BF16)


def close_kernel(keep_a, keep_b, got_a, got_b, last_a, last_b, proj_ref, out_ref, proj_out):
    proj_out[...] = proj_ref[...]
    half = last_a.shape[0]
    out_ref[:half] = (
        keep_a[0].astype(F32) + got_a[0].astype(F32) + last_a[...].astype(F32)
    ).astype(BF16)
    out_ref[half:] = (
        keep_b[0].astype(F32) + got_b[0].astype(F32) + last_b[...].astype(F32)
    ).astype(BF16)


def delta_kernel(
    order_ref, down_ref, coef_ref, base_ref, base_out_ref, turn_ref, after_ref, out_ref, *scratch
):
    del after_ref
    left, right, right_turned, down, sems = scratch
    step = pl.program_id(0)
    wide, feats = out_ref.shape
    count = order_ref.shape[0]

    def copy(k):
        units = pl.ds(pl.multiple_of(order_ref[k] * wide, SPAN), wide)
        return pltpu.make_async_copy(down_ref.at[units], down.at[k], sems.at[k])

    @pl.when(step == 0)
    def _():
        for k in range(count):
            copy(k).start()
        for tile in range(PAD // SPAN):
            lanes = slice(tile * SPAN, (tile + 1) * SPAN)
            sines = slice(PAD + tile * SPAN, PAD + (tile + 1) * SPAN)
            cos, sin = base_ref[0, :, lanes], base_ref[1, :, lanes]
            span_cos, span_sin = span_table(cos, sin)
            for block in range(wide // SPAN):
                at = LOW + MID + block
                c, s = turned(cos[at : at + 1], sin[at : at + 1], span_cos, span_sin)
                units = slice(block * SPAN, (block + 1) * SPAN)
                left[units, lanes] = c.astype(BF16)
                left[units, sines] = s.astype(BF16)
            coef = coef_ref[1:2, lanes] * SCALE_DOWN
            cos, sin = base_out_ref[0, :, lanes], base_out_ref[1, :, lanes]
            span_cos, span_sin = span_table(cos, sin)
            for block in range(feats // SPAN):
                at = LOW + MID + block
                c, s = turned(cos[at : at + 1], sin[at : at + 1], span_cos, span_sin)
                rows = slice(block * SPAN, (block + 1) * SPAN)
                right[0, rows, lanes] = c * coef
                right[1, rows, lanes] = -s * coef

    for tile in range(PAD // SPAN):
        lanes = slice(tile * SPAN, (tile + 1) * SPAN)
        sines = slice(PAD + tile * SPAN, PAD + (tile + 1) * SPAN)
        cos, sin = turn_ref[0, 0:1, lanes], turn_ref[0, 1:2, lanes]
        for rows in (slice(i, i + 64) for i in range(0, feats, 64)):
            c, s = right[0, rows, lanes], right[1, rows, lanes]
            right_turned[rows, lanes] = (cos * c + sin * s).astype(BF16)
            right_turned[rows, sines] = (cos * s - sin * c).astype(BF16)
    delta = against(left[...], right_turned[...])
    copy(step).wait()
    out_ref[...] = (down[step].astype(F32) + delta).astype(BF16)


def summed(ref, first, last):
    total = ref[0, :, first:last].astype(F32)
    for z in range(1, ref.shape[0]):
        total += ref[z, :, first:last].astype(F32)
    return total


def twice(ref, row):
    return jnp.concatenate([ref[row : row + 1], ref[row : row + 1]], axis=1)


def middle_kernel(
    source_ref, sums_ref, proj_ref, coef_ref, base_ref, out_ref, span_ref
):
    rows, lanes_sent = out_ref.shape[1:]
    wide = lanes_sent - SPAN
    blocks = wide // SPAN
    for which in range(2):
        for tile in range(PAD // SPAN):
            lanes = slice(tile * SPAN, (tile + 1) * SPAN)
            c, s = span_table(base_ref[which, 0, :, lanes], base_ref[which, 1, :, lanes])
            span_ref[which, :, lanes] = c.astype(BF16)
            span_ref[which, :, PAD + tile * SPAN : PAD + (tile + 1) * SPAN] = s.astype(BF16)

    def phase(which, block):
        at = slice(LOW + MID + block, LOW + MID + block + 1)
        return base_ref[which, 0, at, :], base_ref[which, 1, at, :]

    def spread(weighted, which, sign):
        by_cos, by_sin = weighted[:, :PAD], sign * weighted[:, PAD:]
        pieces = []
        for block in range(blocks):
            cos, sin = phase(which, block)
            pieces.append(
                jnp.concatenate(
                    [by_cos * cos + by_sin * sin, by_sin * cos - by_cos * sin], axis=1
                ).astype(BF16)
            )
        value = against(jnp.concatenate(pieces, axis=0), span_ref[which])
        return jnp.concatenate(
            [value[block * rows : (block + 1) * rows] for block in range(blocks)], axis=1
        )

    def collect(value, which, sign):
        stacked = jnp.concatenate(
            [value[:, block * SPAN : (block + 1) * SPAN] for block in range(blocks)], axis=0
        )
        found = matmul(stacked, span_ref[which])
        by_cos = jnp.zeros((rows, PAD), F32)
        by_sin = jnp.zeros((rows, PAD), F32)
        for block in range(blocks):
            cos, sin = phase(which, block)
            x = found[block * rows : (block + 1) * rows, :PAD]
            y = found[block * rows : (block + 1) * rows, PAD:]
            by_cos += cos * x - sin * y
            by_sin += sin * x + cos * y
        return by_cos, sign * by_sin

    def kind(k):
        lanes = slice(k * SPAN, (k + 1) * SPAN)
        return [
            proj_ref[source_ref[x], source_ref[4 + c], :, lanes].astype(F32)
            for x in range(proj_ref.shape[0])
            for c in range(proj_ref.shape[1])
        ]

    proj_up = jnp.concatenate(kind(0) + kind(1), axis=1)
    back_down = jnp.concatenate(kind(2) + kind(3), axis=1)
    gate = summed(sums_ref, 0, wide)
    up = summed(sums_ref, wide, 2 * wide) + spread(proj_up * (twice(coef_ref, 0) * SCALE_UP), 0, -1.0)
    dhidden = summed(sums_ref, 2 * wide, 3 * wide) + spread(back_down * (twice(coef_ref, 1) * SCALE_DOWN), 1, 1.0)
    activated = (gate / (1.0 + jnp.exp(-gate))).astype(BF16).astype(F32)
    hidden = (activated * up).astype(BF16)
    dup = (dhidden * activated).astype(BF16)
    up_cos, up_sin = collect(dup, 0, -1.0)
    down_cos, down_sin = collect(hidden, 1, 1.0)

    def over_tokens(value):
        return jnp.sum(value, axis=0, keepdims=True)

    grad_up = SCALE_UP * over_tokens(proj_up[:, :PAD] * up_cos + proj_up[:, PAD:] * up_sin)
    grad_down = SCALE_DOWN * over_tokens(
        down_cos * back_down[:, :PAD] + down_sin * back_down[:, PAD:]
    )
    grads = jnp.concatenate(
        [g[:, k * SPAN : (k + 1) * SPAN] for g in (grad_up, grad_down) for k in range(PAD // SPAN)],
        axis=0,
    ).astype(BF16)
    for c in range(out_ref.shape[0]):
        out_ref[c, :, :wide] = hidden
        out_ref[c, :, wide:] = grads


def regroup_kernel(in_ref, out_ref):
    peers, rows, _ = in_ref.shape
    wide = out_ref.shape[1]
    grads = jnp.zeros((rows, SPAN), F32)
    for z in range(peers):
        out_ref[z * rows : (z + 1) * rows, :] = in_ref[z, :, :wide]
        grads += in_ref[z, :, wide:].astype(F32)
    high, low = split(grads)
    out_ref[peers * rows :, :SPAN] = high
    out_ref[peers * rows :, SPAN : 2 * SPAN] = low
    out_ref[peers * rows :, 2 * SPAN :] = jnp.zeros((rows, wide - 2 * SPAN), BF16)


def last_kernel(own_ref, one_ref, two_ref, three_ref, weight_ref, out_ref):
    peers, rows, feats = out_ref.shape
    rows //= 2
    wide = own_ref.shape[1]
    count = peers * rows
    total = jnp.zeros((count, feats), F32)
    grads = jnp.zeros((own_ref.shape[0] - count, SPAN), F32)
    for k, ref in enumerate((own_ref, one_ref, two_ref, three_ref)):
        units = slice(k * wide, (k + 1) * wide)
        total += matmul(ref[:count, :], weight_ref[units, :])
        grads += ref[count:, :SPAN].astype(F32) + ref[count:, SPAN : 2 * SPAN].astype(F32)
    high, low = split(grads)
    for r in range(peers):
        out_ref[r, :rows, :] = total[r * rows : (r + 1) * rows, :].astype(BF16)
        out_ref[r, rows:, :SPAN] = high
        out_ref[r, rows:, SPAN:] = low


def update_kernel(in_ref, first_ref, second_ref, mixed_ref, step_ref, scratch):
    peers, rows, _ = in_ref.shape
    rows //= 2
    mixed = jnp.zeros(mixed_ref.shape, F32)
    pieces = jnp.zeros((rows, SPAN), F32)
    for r in range(peers):
        mixed += in_ref[r, :rows, :].astype(F32)
        pieces += in_ref[r, rows:, :SPAN].astype(F32)
        pieces += in_ref[r, rows:, SPAN:].astype(F32)
    mixed_ref[...] = mixed.astype(BF16)
    per = PAD // SPAN
    for k in range(rows):
        at = k % per
        scratch[k // per : k // per + 1, at * SPAN : (at + 1) * SPAN] = pieces[k : k + 1]
    grads = scratch[:, :N_COEF]
    squares = jnp.sum(jnp.sum(grads * grads, axis=1, keepdims=True), axis=0, keepdims=True)
    norm_value = jnp.sqrt(squares)
    clipped = grads * jnp.minimum(1.0, 1.0 / (norm_value + 1e-06))
    first = 0.9 * first_ref[...] + 0.1 * clipped
    second = 0.999 * second_ref[...] + 0.001 * clipped * clipped
    step_ref[...] = (
        first / (1.0 - 0.9**ADAM_STEP) / (jnp.sqrt(second / (1.0 - 0.999**ADAM_STEP)) + 1e-08)
    )


def on_device(
    tokens,
    cotangent,
    gate_weight,
    up_weight,
    down_weight,
    coefficients,
    spectral_rows,
    spectral_cols,
    adam_first,
    adam_second,
):
    peers_row = lax.axis_size(PLANE)
    peers_z = lax.axis_size("z")
    peers_y = lax.axis_size("y")
    row_index = lax.axis_index(PLANE)
    z_index = lax.axis_index("z")
    y_index = lax.axis_index("y")
    own, feats = tokens.shape
    units = gate_weight.shape[1]
    wide = units // peers_y
    count = own * peers_row
    feat_first = (z_index * peers_y + y_index) * feats
    unit_first = row_index * units

    def exchange(value, axes):
        return lax.all_to_all(value, axes, 0, 0, tiled=True)

    def padded(values):
        return jnp.pad(values, (0, PAD - N_COEF))

    lanes = row_index * SPAN
    own_left = lax.dynamic_slice_in_dim(padded(spectral_rows[0]), lanes, SPAN)
    own_right = lax.dynamic_slice_in_dim(padded(spectral_cols[1]), lanes, SPAN)
    base_own = jnp.stack(
        [
            phases(own_left, feat_first, feats // SPAN, D),
            phases(own_right, feat_first, feats // SPAN, D),
        ]
    )

    both = pl.pallas_call(
        spread_kernel,
        in_specs=[VMEM] * 2,
        out_specs=VMEM,
        out_shape=jax.ShapeDtypeStruct((peers_row, own, 2 * feats), BF16),
    )(tokens, cotangent)
    both = exchange(both, PLANE).reshape(count, 2 * feats)

    share = count // peers_z
    half = count // 2
    block = 3 * wide
    smem = pl.BlockSpec(memory_space=pltpu.SMEM)
    hbm = pl.BlockSpec(memory_space=pltpu.HBM)
    anywhere = pl.BlockSpec(memory_space=pl.ANY)
    order = y_index ^ jnp.array([1, 2, 3, 0], jnp.int32)
    pieces = jax.ShapeDtypeStruct((2, half, block), BF16)

    def full(shape):
        return pl.BlockSpec(shape, lambda i: (0,) * len(shape))

    table = pl.pallas_call(
        own_table_kernel,
        in_specs=[VMEM],
        out_specs=VMEM,
        out_shape=jax.ShapeDtypeStruct((2, feats, 2 * SPAN), BF16),
        compiler_params=params(8),
    )(base_own)
    send_a, send_b, keep_a, keep_b = pl.pallas_call(
        first_kernel,
        in_specs=[smem, VMEM, hbm, hbm, hbm],
        out_specs=[VMEM] * 4,
        out_shape=[pieces] * 4,
        scratch_shapes=[
            pltpu.VMEM((peers_y, feats, wide), BF16),
            pltpu.VMEM((peers_y, feats, wide), BF16),
            pltpu.VMEM((peers_y, wide, feats), BF16),
            pltpu.SemaphoreType.DMA((peers_y, 3)),
        ],
        compiler_params=params(60),
    )(order, both, gate_weight, up_weight, down_weight)

    def swap(value, mask):
        return lax.ppermute(value, "y", [(y, y ^ mask) for y in range(peers_y)])

    got_a, got_b = swap(send_a, 1), swap(send_b, 3)
    proj = pl.pallas_call(
        project_kernel,
        in_specs=[VMEM] * 2 + [anywhere],
        out_specs=VMEM,
        out_shape=jax.ShapeDtypeStruct((count, peers_y * SPAN), BF16),
        compiler_params=params(8),
    )(both, table, keep_a)
    proj = exchange(proj.reshape(peers_z, share, peers_y * SPAN), "z")

    freq, coefs = pl.pallas_call(
        late_kernel,
        in_specs=[VMEM] * 3 + [anywhere],
        out_specs=[VMEM] * 2,
        out_shape=[
            jax.ShapeDtypeStruct((4, PAD), jnp.int32),
            jax.ShapeDtypeStruct((2, PAD), F32),
        ],
    )(spectral_rows, spectral_cols, coefficients, keep_a)
    tile_first = unit_first + y_index * wide
    base_up = phases(freq[2], tile_first, wide // SPAN, FF)
    base_down = phases(freq[1], tile_first, wide // SPAN, FF)
    base_out = phases(freq[3], feat_first, feats // SPAN, D)
    sources = (y_index - jnp.arange(peers_y, dtype=jnp.int32)) & 3
    turns = waves(((sources - y_index) * wide)[:, None], freq[1], FF, 1)
    turns = turns.reshape(peers_y, 2, PAD)

    def added(values):
        return pl.pallas_call(
            sum_kernel,
            in_specs=[VMEM] * len(values),
            out_specs=VMEM,
            out_shape=jax.ShapeDtypeStruct(values[0].shape, BF16),
            compiler_params=params(8),
        )(*values)

    def turn(value, axis, peers, k):
        return lax.ppermute(value, axis, [(i, (i + k) % peers) for i in range(peers)])

    proj = jnp.sum(proj.astype(F32), axis=0).astype(BF16)
    proj = added([proj] + [turn(proj, "y", peers_y, k) for k in (1, 2, 3)])
    def whole(rows):
        return pl.BlockSpec((1, half, block), lambda i: (rows, 0, 0))

    send_a, send_b = pl.pallas_call(
        fold_kernel,
        grid=(1,),
        in_specs=[whole(0), whole(0), whole(1), whole(0)],
        out_specs=[full((half, block))] * 2,
        out_shape=[jax.ShapeDtypeStruct((half, block), BF16)] * 2,
        compiler_params=params(12),
    )(keep_a, keep_b, got_a, got_b)
    last_a, last_b = swap(send_a, 3), swap(send_b, 1)
    sums, proj = pl.pallas_call(
        close_kernel,
        grid=(1,),
        in_specs=[whole(1), whole(1), whole(0), whole(1)] + [full((half, block))] * 2
        + [full(proj.shape)],
        out_specs=[full((count, block)), full(proj.shape)],
        out_shape=[
            jax.ShapeDtypeStruct((count, block), BF16),
            jax.ShapeDtypeStruct(proj.shape, BF16),
        ],
        compiler_params=params(12),
    )(keep_a, keep_b, got_a, got_b, last_a, last_b, proj)
    proj = jnp.stack([proj, lax.ppermute(proj, "core", [(0, 1), (1, 0)])])
    proj = jnp.stack([proj] + [turn(proj, "x", 4, k) for k in (1, 2, 3)])
    chip = (lax.axis_index("x") - jnp.arange(4, dtype=jnp.int32)) & 3
    core = lax.axis_index("core") ^ jnp.arange(2, dtype=jnp.int32)
    source = jnp.concatenate([chip, core])
    sums = exchange(sums.reshape(peers_z, share, block), "z")

    hidden = pl.pallas_call(
        middle_kernel,
        in_specs=[smem] + [VMEM] * 4,
        out_specs=VMEM,
        out_shape=jax.ShapeDtypeStruct((peers_z, share, wide + SPAN), BF16),
        scratch_shapes=[pltpu.VMEM((2, SPAN, 2 * PAD), BF16)],
        compiler_params=params(12),
    )(source, sums, proj, coefs, jnp.stack([base_up, base_down]))
    hidden = exchange(hidden, "z")
    hidden = pl.pallas_call(
        regroup_kernel,
        in_specs=[VMEM],
        out_specs=VMEM,
        out_shape=jax.ShapeDtypeStruct((count + share, wide), BF16),
        compiler_params=params(8),
    )(hidden)
    weight = pl.pallas_call(
        delta_kernel,
        grid=(peers_y,),
        in_specs=[
            smem,
            hbm,
            full(coefs.shape),
            full(base_down.shape),
            full(base_out.shape),
            pl.BlockSpec((1,) + turns.shape[1:], lambda i: (i, 0, 0)),
            anywhere,
        ],
        out_specs=pl.BlockSpec((wide, feats), lambda i: (i, 0)),
        out_shape=jax.ShapeDtypeStruct((units, feats), BF16),
        scratch_shapes=[
            pltpu.VMEM((wide, 2 * PAD), BF16),
            pltpu.VMEM((2, feats, PAD), F32),
            pltpu.VMEM((feats, 2 * PAD), BF16),
            pltpu.VMEM((peers_y, wide, feats), BF16),
            pltpu.SemaphoreType.DMA((peers_y,)),
        ],
        compiler_params=params(20),
        cost_estimate=pl.CostEstimate(
            flops=6 << 30, bytes_accessed=8 << 20, transcendentals=0
        ),
    )(sources, down_weight, coefs, base_down, base_out, turns, hidden)

    def shifted(k):
        return lax.ppermute(hidden, "y", [(y, (y + k) % peers_y) for y in range(peers_y)])

    others = [shifted(1), shifted(2), shifted(3)]
    mixed = pl.pallas_call(
        last_kernel,
        in_specs=[VMEM] * 5,
        out_specs=VMEM,
        out_shape=jax.ShapeDtypeStruct((peers_row, 2 * own, feats), BF16),
        compiler_params=params(12),
    )(hidden, *others, weight)
    mixed = exchange(mixed, PLANE)

    return pl.pallas_call(
        update_kernel,
        in_specs=[VMEM] * 3,
        out_specs=[VMEM] * 2,
        out_shape=[
            jax.ShapeDtypeStruct((own, feats), BF16),
            jax.ShapeDtypeStruct(adam_first.shape, F32),
        ],
        scratch_shapes=[pltpu.VMEM((2, PAD), F32)],
    )(mixed, adam_first, adam_second)


def solution(mesh):
    chips = Mesh(mesh.devices.reshape(4, 2, 8, 4), ("x", "core", "z", "y"))
    tiles = P(("x", "core"), ("z", "y"))
    weights = P(("z", "y"), ("x", "core"))
    placed = (tiles, tiles, weights, weights, tiles, P(), P(), P(), P(), P())
    return jax.shard_map(
        on_device, mesh=chips, in_specs=placed, out_specs=(tiles, P()), check_vma=False
    )
```

```python
import math

import jax
import jax.numpy as jnp
from jax import lax
from jax.experimental import pallas as pl
from jax.experimental.pallas import tpu as pltpu
from jax.sharding import Mesh
from jax.sharding import PartitionSpec as P

D = 8192
FF = 28672
N_COEF = 1000
ADAM_STEP = 3
PAD = 1024
SCALE_UP = 1.0 / math.sqrt(2.0 * D * N_COEF)
SCALE_DOWN = 1.0 / math.sqrt(2.0 * FF * N_COEF)
TWO_PI = 6.283185307179586

F32 = jnp.float32
BF16 = jnp.bfloat16
LOW = 8
MID = 16
SPAN = LOW * MID

PLANE = ("x", "core")
VMEM = pl.BlockSpec(memory_space=pltpu.VMEM)


def params(mib):
    return pltpu.CompilerParams(vmem_limit_bytes=mib << 20)


def waves(index, freq, width, axis):
    phase = index[..., None] * freq % width
    angle = phase.astype(F32) * (TWO_PI / width)
    return jnp.stack([jnp.cos(angle), jnp.sin(angle)], axis=axis)


def phases(freq, first, blocks, width):
    rows = -(-(LOW + MID + blocks) // 8) * 8
    index = jnp.concatenate(
        [
            jnp.arange(LOW, dtype=jnp.int32),
            LOW * jnp.arange(MID, dtype=jnp.int32),
            first + SPAN * jnp.arange(blocks, dtype=jnp.int32),
            jnp.zeros(rows - LOW - MID - blocks, jnp.int32),
        ]
    )
    return waves(index, freq, width, 0)


def span_table(cos, sin):
    low_cos, low_sin = cos[:LOW], sin[:LOW]
    out_cos, out_sin = [], []
    for k in range(MID):
        a, b = cos[LOW + k : LOW + k + 1], sin[LOW + k : LOW + k + 1]
        out_cos.append(a * low_cos - b * low_sin)
        out_sin.append(b * low_cos + a * low_sin)
    return jnp.concatenate(out_cos, axis=0), jnp.concatenate(out_sin, axis=0)


def turned(cos, sin, span_cos, span_sin):
    return cos * span_cos - sin * span_sin, sin * span_cos + cos * span_sin


def against(left, table):
    return lax.dot_general(
        left, table, (((1,), (1,)), ((), ())), preferred_element_type=F32
    )


def matmul(left, right):
    return jnp.dot(left, right, preferred_element_type=F32)


def split(value):
    high = value.astype(BF16)
    return high, (value - high.astype(F32)).astype(BF16)


def spread_kernel(tokens_ref, cotangent_ref, out_ref):
    feats = tokens_ref.shape[1]
    for r in range(out_ref.shape[0]):
        out_ref[r, :, :feats] = tokens_ref[...]
        out_ref[r, :, feats:] = cotangent_ref[...]


def own_table_kernel(base_ref, out_ref):
    for which, sign in ((0, 1.0), (1, -1.0)):
        cos, sin = base_ref[which, 0], base_ref[which, 1]
        span_cos, span_sin = span_table(cos, sin)
        for block in range(out_ref.shape[1] // SPAN):
            at = LOW + MID + block
            c, s = turned(cos[at : at + 1], sin[at : at + 1], span_cos, span_sin)
            rows = slice(block * SPAN, (block + 1) * SPAN)
            out_ref[which, rows, :SPAN] = c.astype(BF16)
            out_ref[which, rows, SPAN:] = (sign * s).astype(BF16)


def late_kernel(rows_ref, cols_ref, coef_ref, after_ref, freq_ref, coef_out):
    del after_ref
    freq_ref[...] = jnp.zeros(freq_ref.shape, jnp.int32)
    coef_out[...] = jnp.zeros(coef_out.shape, F32)
    freq_ref[0:2, :N_COEF] = rows_ref[...]
    freq_ref[2:4, :N_COEF] = cols_ref[...]
    coef_out[:, :N_COEF] = coef_ref[...]


def sum_kernel(*refs):
    total = refs[0][...].astype(F32)
    for ref in refs[1:-1]:
        total += ref[...].astype(F32)
    refs[-1][...] = total.astype(BF16)


def quarter_copies(order_ref, refs, scratch, sems, first):
    wide = scratch[0].shape[2]
    copies = []
    for i in range(scratch[0].shape[0]):
        units = pl.ds(pl.multiple_of(order_ref[first + i] * wide, SPAN), wide)
        places = (refs[0].at[:, units], refs[1].at[:, units], refs[2].at[units, :])
        copies.append(
            [
                pltpu.make_async_copy(place, to.at[i], sems.at[i, k])
                for k, (place, to) in enumerate(zip(places, scratch, strict=True))
            ]
        )
    for three in copies:
        for copy in three:
            copy.start()
    return copies


def quarter_parts(x_ref, scratch, i, copies):
    feats = x_ref.shape[1] // 2
    for copy in copies[i]:
        copy.wait()
    gates, ups, downs = scratch
    tokens, cotangent = x_ref[:, :feats], x_ref[:, feats:]
    return matmul(tokens, gates[i]), matmul(tokens, ups[i]), against(cotangent, downs[i])


def first_kernel(
    order_ref, x_ref, gate_ref, up_ref, down_ref, send_a, send_b, keep_a, keep_b, *scratch
):
    *scratch, sems = scratch
    copies = quarter_copies(order_ref, (gate_ref, up_ref, down_ref), scratch, sems, 0)
    half, wide = x_ref.shape[0] // 2, scratch[0].shape[2]
    places = (
        (send_a.at[0], keep_b),
        (send_a.at[1], send_b.at[0]),
        (keep_a, send_b.at[1]),
    )
    for i, (low, high) in enumerate(places):
        for at, part in enumerate(quarter_parts(x_ref, scratch, i, copies)):
            lanes = slice(at * wide, (at + 1) * wide)
            low[:, lanes] = part[:half].astype(BF16)
            high[:, lanes] = part[half:].astype(BF16)


def own_kernel(
    order_ref, x_ref, table_ref, gate_ref, up_ref, down_ref, after_ref, proj_ref, own_ref, *scratch
):
    del after_ref
    *scratch, sems = scratch
    copies = quarter_copies(order_ref, (gate_ref, up_ref, down_ref), scratch, sems, 3)
    feats, wide = scratch[0].shape[1:]
    for which in range(2):
        values = x_ref[:, which * feats : (which + 1) * feats]
        lanes = slice(2 * which * SPAN, 2 * (which + 1) * SPAN)
        proj_ref[:, lanes] = matmul(values, table_ref[which]).astype(BF16)
    for at, part in enumerate(quarter_parts(x_ref, scratch, 0, copies)):
        own_ref[:, at * wide : (at + 1) * wide] = part.astype(BF16)


def fold_kernel(keep_a, keep_b, got_a, got_b, after_ref, send_a, send_b):
    del after_ref
    send_a[...] = (keep_a[...].astype(F32) + got_a[0].astype(F32)).astype(BF16)
    send_b[...] = (keep_b[...].astype(F32) + got_b[0].astype(F32)).astype(BF16)


def close_kernel(own_ref, got_a, got_b, last_a, last_b, proj_ref, out_ref, proj_out):
    proj_out[...] = proj_ref[...]
    half = last_a.shape[0]
    out_ref[:half] = (
        own_ref[:half].astype(F32) + got_a[0].astype(F32) + last_a[...].astype(F32)
    ).astype(BF16)
    out_ref[half:] = (
        own_ref[half:].astype(F32) + got_b[0].astype(F32) + last_b[...].astype(F32)
    ).astype(BF16)


def delta_kernel(
    order_ref, down_ref, coef_ref, base_ref, base_out_ref, turn_ref, after_ref, out_ref, *scratch
):
    del after_ref
    left, right, right_turned, down, sems = scratch
    step = pl.program_id(0)
    wide, feats = out_ref.shape
    count = order_ref.shape[0]

    def copy(k):
        units = pl.ds(pl.multiple_of(order_ref[k] * wide, SPAN), wide)
        return pltpu.make_async_copy(down_ref.at[units], down.at[k], sems.at[k])

    @pl.when(step == 0)
    def _():
        for k in range(count):
            copy(k).start()
        for tile in range(PAD // SPAN):
            lanes = slice(tile * SPAN, (tile + 1) * SPAN)
            sines = slice(PAD + tile * SPAN, PAD + (tile + 1) * SPAN)
            cos, sin = base_ref[0, :, lanes], base_ref[1, :, lanes]
            span_cos, span_sin = span_table(cos, sin)
            for block in range(wide // SPAN):
                at = LOW + MID + block
                c, s = turned(cos[at : at + 1], sin[at : at + 1], span_cos, span_sin)
                units = slice(block * SPAN, (block + 1) * SPAN)
                left[units, lanes] = c.astype(BF16)
                left[units, sines] = s.astype(BF16)
            coef = coef_ref[1:2, lanes] * SCALE_DOWN
            cos, sin = base_out_ref[0, :, lanes], base_out_ref[1, :, lanes]
            span_cos, span_sin = span_table(cos, sin)
            for block in range(feats // SPAN):
                at = LOW + MID + block
                c, s = turned(cos[at : at + 1], sin[at : at + 1], span_cos, span_sin)
                rows = slice(block * SPAN, (block + 1) * SPAN)
                right[0, rows, lanes] = c * coef
                right[1, rows, lanes] = -s * coef

    for tile in range(PAD // SPAN):
        lanes = slice(tile * SPAN, (tile + 1) * SPAN)
        sines = slice(PAD + tile * SPAN, PAD + (tile + 1) * SPAN)
        cos, sin = turn_ref[0, 0:1, lanes], turn_ref[0, 1:2, lanes]
        for rows in (slice(i, i + 64) for i in range(0, feats, 64)):
            c, s = right[0, rows, lanes], right[1, rows, lanes]
            right_turned[rows, lanes] = (cos * c + sin * s).astype(BF16)
            right_turned[rows, sines] = (cos * s - sin * c).astype(BF16)
    delta = against(left[...], right_turned[...])
    copy(step).wait()
    out_ref[...] = (down[step].astype(F32) + delta).astype(BF16)


def summed(ref, first, last):
    total = ref[0, :, first:last].astype(F32)
    for z in range(1, ref.shape[0]):
        total += ref[z, :, first:last].astype(F32)
    return total


def twice(ref, row):
    return jnp.concatenate([ref[row : row + 1], ref[row : row + 1]], axis=1)


def middle_kernel(
    source_ref, sums_ref, proj_ref, coef_ref, base_ref, out_ref, span_ref
):
    rows, lanes_sent = out_ref.shape[1:]
    wide = lanes_sent - SPAN
    blocks = wide // SPAN
    for which in range(2):
        for tile in range(PAD // SPAN):
            lanes = slice(tile * SPAN, (tile + 1) * SPAN)
            c, s = span_table(base_ref[which, 0, :, lanes], base_ref[which, 1, :, lanes])
            span_ref[which, :, lanes] = c.astype(BF16)
            span_ref[which, :, PAD + tile * SPAN : PAD + (tile + 1) * SPAN] = s.astype(BF16)

    def phase(which, block):
        at = slice(LOW + MID + block, LOW + MID + block + 1)
        return base_ref[which, 0, at, :], base_ref[which, 1, at, :]

    def spread(weighted, which, sign):
        by_cos, by_sin = weighted[:, :PAD], sign * weighted[:, PAD:]
        pieces = []
        for block in range(blocks):
            cos, sin = phase(which, block)
            pieces.append(
                jnp.concatenate(
                    [by_cos * cos + by_sin * sin, by_sin * cos - by_cos * sin], axis=1
                ).astype(BF16)
            )
        value = against(jnp.concatenate(pieces, axis=0), span_ref[which])
        return jnp.concatenate(
            [value[block * rows : (block + 1) * rows] for block in range(blocks)], axis=1
        )

    def collect(value, which, sign):
        stacked = jnp.concatenate(
            [value[:, block * SPAN : (block + 1) * SPAN] for block in range(blocks)], axis=0
        )
        found = matmul(stacked, span_ref[which])
        by_cos = jnp.zeros((rows, PAD), F32)
        by_sin = jnp.zeros((rows, PAD), F32)
        for block in range(blocks):
            cos, sin = phase(which, block)
            x = found[block * rows : (block + 1) * rows, :PAD]
            y = found[block * rows : (block + 1) * rows, PAD:]
            by_cos += cos * x - sin * y
            by_sin += sin * x + cos * y
        return by_cos, sign * by_sin

    def kind(k):
        lanes = slice(k * SPAN, (k + 1) * SPAN)
        return [
            proj_ref[source_ref[x], source_ref[4 + c], :, lanes].astype(F32)
            for x in range(proj_ref.shape[0])
            for c in range(proj_ref.shape[1])
        ]

    proj_up = jnp.concatenate(kind(0) + kind(1), axis=1)
    back_down = jnp.concatenate(kind(2) + kind(3), axis=1)
    gate = summed(sums_ref, 0, wide)
    up = summed(sums_ref, wide, 2 * wide) + spread(proj_up * (twice(coef_ref, 0) * SCALE_UP), 0, -1.0)
    dhidden = summed(sums_ref, 2 * wide, 3 * wide) + spread(back_down * (twice(coef_ref, 1) * SCALE_DOWN), 1, 1.0)
    activated = (gate / (1.0 + jnp.exp(-gate))).astype(BF16).astype(F32)
    hidden = (activated * up).astype(BF16)
    dup = (dhidden * activated).astype(BF16)
    up_cos, up_sin = collect(dup, 0, -1.0)
    down_cos, down_sin = collect(hidden, 1, 1.0)

    def over_tokens(value):
        return jnp.sum(value, axis=0, keepdims=True)

    grad_up = SCALE_UP * over_tokens(proj_up[:, :PAD] * up_cos + proj_up[:, PAD:] * up_sin)
    grad_down = SCALE_DOWN * over_tokens(
        down_cos * back_down[:, :PAD] + down_sin * back_down[:, PAD:]
    )
    grads = jnp.concatenate(
        [g[:, k * SPAN : (k + 1) * SPAN] for g in (grad_up, grad_down) for k in range(PAD // SPAN)],
        axis=0,
    ).astype(BF16)
    for c in range(out_ref.shape[0]):
        out_ref[c, :, :wide] = hidden
        out_ref[c, :, wide:] = grads


def regroup_kernel(in_ref, after_ref, out_ref):
    del after_ref
    peers, rows, _ = in_ref.shape
    wide = out_ref.shape[1]
    grads = jnp.zeros((rows, SPAN), F32)
    for z in range(peers):
        out_ref[z * rows : (z + 1) * rows, :] = in_ref[z, :, :wide]
        grads += in_ref[z, :, wide:].astype(F32)
    high, low = split(grads)
    out_ref[peers * rows :, :SPAN] = high
    out_ref[peers * rows :, SPAN : 2 * SPAN] = low
    out_ref[peers * rows :, 2 * SPAN :] = jnp.zeros((rows, wide - 2 * SPAN), BF16)


def last_kernel(own_ref, one_ref, two_ref, three_ref, near_ref, far_ref, out_ref):
    peers, rows, feats = out_ref.shape
    rows //= 2
    wide = own_ref.shape[1]
    count = peers * rows
    total = jnp.zeros((count, feats), F32)
    grads = jnp.zeros((own_ref.shape[0] - count, SPAN), F32)
    for k, ref in enumerate((own_ref, one_ref, two_ref, three_ref)):
        weight_ref = (near_ref, far_ref)[k // 2]
        units = slice(k % 2 * wide, (k % 2 + 1) * wide)
        total += matmul(ref[:count, :], weight_ref[units, :])
        grads += ref[count:, :SPAN].astype(F32) + ref[count:, SPAN : 2 * SPAN].astype(F32)
    high, low = split(grads)
    for r in range(peers):
        out_ref[r, :rows, :] = total[r * rows : (r + 1) * rows, :].astype(BF16)
        out_ref[r, rows:, :SPAN] = high
        out_ref[r, rows:, SPAN:] = low


def update_kernel(in_ref, first_ref, second_ref, mixed_ref, step_ref, scratch):
    peers, rows, _ = in_ref.shape
    rows //= 2
    mixed = jnp.zeros(mixed_ref.shape, F32)
    pieces = jnp.zeros((rows, SPAN), F32)
    for r in range(peers):
        mixed += in_ref[r, :rows, :].astype(F32)
        pieces += in_ref[r, rows:, :SPAN].astype(F32)
        pieces += in_ref[r, rows:, SPAN:].astype(F32)
    mixed_ref[...] = mixed.astype(BF16)
    per = PAD // SPAN
    for k in range(rows):
        at = k % per
        scratch[k // per : k // per + 1, at * SPAN : (at + 1) * SPAN] = pieces[k : k + 1]
    grads = scratch[:, :N_COEF]
    squares = jnp.sum(jnp.sum(grads * grads, axis=1, keepdims=True), axis=0, keepdims=True)
    norm_value = jnp.sqrt(squares)
    clipped = grads * jnp.minimum(1.0, 1.0 / (norm_value + 1e-06))
    first = 0.9 * first_ref[...] + 0.1 * clipped
    second = 0.999 * second_ref[...] + 0.001 * clipped * clipped
    step_ref[...] = (
        first / (1.0 - 0.9**ADAM_STEP) / (jnp.sqrt(second / (1.0 - 0.999**ADAM_STEP)) + 1e-08)
    )


def on_device(
    tokens,
    cotangent,
    gate_weight,
    up_weight,
    down_weight,
    coefficients,
    spectral_rows,
    spectral_cols,
    adam_first,
    adam_second,
):
    peers_row = lax.axis_size(PLANE)
    peers_z = lax.axis_size("z")
    peers_y = lax.axis_size("y")
    row_index = lax.axis_index(PLANE)
    z_index = lax.axis_index("z")
    y_index = lax.axis_index("y")
    own, feats = tokens.shape
    units = gate_weight.shape[1]
    wide = units // peers_y
    count = own * peers_row
    feat_first = (z_index * peers_y + y_index) * feats
    unit_first = row_index * units

    def exchange(value, axes):
        return lax.all_to_all(value, axes, 0, 0, tiled=True)

    def padded(values):
        return jnp.pad(values, (0, PAD - N_COEF))

    lanes = row_index * SPAN
    own_left = lax.dynamic_slice_in_dim(padded(spectral_rows[0]), lanes, SPAN)
    own_right = lax.dynamic_slice_in_dim(padded(spectral_cols[1]), lanes, SPAN)
    base_own = jnp.stack(
        [
            phases(own_left, feat_first, feats // SPAN, D),
            phases(own_right, feat_first, feats // SPAN, D),
        ]
    )

    both = pl.pallas_call(
        spread_kernel,
        in_specs=[VMEM] * 2,
        out_specs=VMEM,
        out_shape=jax.ShapeDtypeStruct((peers_row, own, 2 * feats), BF16),
    )(tokens, cotangent)
    both = exchange(both, PLANE).reshape(count, 2 * feats)

    share = count // peers_z
    half = count // 2
    block = 3 * wide
    smem = pl.BlockSpec(memory_space=pltpu.SMEM)
    hbm = pl.BlockSpec(memory_space=pltpu.HBM)
    anywhere = pl.BlockSpec(memory_space=pl.ANY)
    order = y_index ^ jnp.array([1, 2, 3, 0], jnp.int32)
    pieces = jax.ShapeDtypeStruct((2, half, block), BF16)

    def full(shape):
        return pl.BlockSpec(shape, lambda i: (0,) * len(shape))

    table = pl.pallas_call(
        own_table_kernel,
        in_specs=[VMEM],
        out_specs=VMEM,
        out_shape=jax.ShapeDtypeStruct((2, feats, 2 * SPAN), BF16),
        compiler_params=params(8),
    )(base_own)
    def scratch(quarters):
        return [
            pltpu.VMEM((quarters, feats, wide), BF16),
            pltpu.VMEM((quarters, feats, wide), BF16),
            pltpu.VMEM((quarters, wide, feats), BF16),
            pltpu.SemaphoreType.DMA((quarters, 3)),
        ]

    piece = jax.ShapeDtypeStruct((half, block), BF16)
    send_a, send_b, keep_a, keep_b = pl.pallas_call(
        first_kernel,
        in_specs=[smem, VMEM, hbm, hbm, hbm],
        out_specs=[VMEM] * 4,
        out_shape=[pieces] * 2 + [piece] * 2,
        scratch_shapes=scratch(peers_y - 1),
        compiler_params=params(57),
    )(order, both, gate_weight, up_weight, down_weight)

    def swap(value, mask):
        return lax.ppermute(value, "y", [(y, y ^ mask) for y in range(peers_y)])

    got_a, got_b = swap(send_a, 1), swap(send_b, 3)
    proj, mine = pl.pallas_call(
        own_kernel,
        in_specs=[smem, VMEM, VMEM, hbm, hbm, hbm, anywhere],
        out_specs=[VMEM] * 2,
        out_shape=[
            jax.ShapeDtypeStruct((count, peers_y * SPAN), BF16),
            jax.ShapeDtypeStruct((count, block), BF16),
        ],
        scratch_shapes=scratch(1),
        compiler_params=params(57),
    )(order, both, table, gate_weight, up_weight, down_weight, keep_a)
    proj = exchange(proj.reshape(peers_z, share, peers_y * SPAN), "z")

    freq, coefs = pl.pallas_call(
        late_kernel,
        in_specs=[VMEM] * 3 + [anywhere],
        out_specs=[VMEM] * 2,
        out_shape=[
            jax.ShapeDtypeStruct((4, PAD), jnp.int32),
            jax.ShapeDtypeStruct((2, PAD), F32),
        ],
    )(spectral_rows, spectral_cols, coefficients, keep_a)
    tile_first = unit_first + y_index * wide
    base_up = phases(freq[2], tile_first, wide // SPAN, FF)
    base_down = phases(freq[1], tile_first, wide // SPAN, FF)
    base_out = phases(freq[3], feat_first, feats // SPAN, D)
    sources = (y_index - jnp.arange(peers_y, dtype=jnp.int32)) & 3
    turns = waves(((sources - y_index) * wide)[:, None], freq[1], FF, 1)
    turns = turns.reshape(peers_y, 2, PAD)

    def added(values):
        return pl.pallas_call(
            sum_kernel,
            in_specs=[VMEM] * len(values),
            out_specs=VMEM,
            out_shape=jax.ShapeDtypeStruct(values[0].shape, BF16),
            compiler_params=params(8),
        )(*values)

    def turn(value, axis, peers, k):
        return lax.ppermute(value, axis, [(i, (i + k) % peers) for i in range(peers)])

    proj = jnp.sum(proj.astype(F32), axis=0).astype(BF16)
    proj = added([proj] + [turn(proj, "y", peers_y, k) for k in (1, 2, 3)])
    def whole(rows):
        return pl.BlockSpec((1, half, block), lambda i: (rows, 0, 0))

    send_a, send_b = pl.pallas_call(
        fold_kernel,
        grid=(1,),
        in_specs=[full((half, block))] * 2 + [whole(1), whole(0), anywhere],
        out_specs=[full((half, block))] * 2,
        out_shape=[jax.ShapeDtypeStruct((half, block), BF16)] * 2,
        compiler_params=params(12),
    )(keep_a, keep_b, got_a, got_b, freq)
    last_a, last_b = swap(send_a, 3), swap(send_b, 1)
    sums, proj = pl.pallas_call(
        close_kernel,
        grid=(1,),
        in_specs=[full((count, block)), whole(0), whole(1)] + [full((half, block))] * 2
        + [full(proj.shape)],
        out_specs=[full((count, block)), full(proj.shape)],
        out_shape=[
            jax.ShapeDtypeStruct((count, block), BF16),
            jax.ShapeDtypeStruct(proj.shape, BF16),
        ],
        compiler_params=params(12),
    )(mine, got_a, got_b, last_a, last_b, proj)
    proj = jnp.stack([proj, lax.ppermute(proj, "core", [(0, 1), (1, 0)])])
    proj = jnp.stack([proj] + [turn(proj, "x", 4, k) for k in (1, 2, 3)])
    chip = (lax.axis_index("x") - jnp.arange(4, dtype=jnp.int32)) & 3
    core = lax.axis_index("core") ^ jnp.arange(2, dtype=jnp.int32)
    source = jnp.concatenate([chip, core])
    sums = exchange(sums.reshape(peers_z, share, block), "z")

    hidden = pl.pallas_call(
        middle_kernel,
        in_specs=[smem] + [VMEM] * 4,
        out_specs=VMEM,
        out_shape=jax.ShapeDtypeStruct((peers_z, share, wide + SPAN), BF16),
        scratch_shapes=[pltpu.VMEM((2, SPAN, 2 * PAD), BF16)],
        compiler_params=params(12),
    )(source, sums, proj, coefs, jnp.stack([base_up, base_down]))
    def updated(first, after):
        return pl.pallas_call(
            delta_kernel,
            grid=(2,),
            in_specs=[
                smem,
                hbm,
                full(coefs.shape),
                full(base_down.shape),
                full(base_out.shape),
                pl.BlockSpec((1,) + turns.shape[1:], lambda i: (i, 0, 0)),
                anywhere,
            ],
            out_specs=pl.BlockSpec((wide, feats), lambda i: (i, 0)),
            out_shape=jax.ShapeDtypeStruct((2 * wide, feats), BF16),
            scratch_shapes=[
                pltpu.VMEM((wide, 2 * PAD), BF16),
                pltpu.VMEM((2, feats, PAD), F32),
                pltpu.VMEM((feats, 2 * PAD), BF16),
                pltpu.VMEM((2, wide, feats), BF16),
                pltpu.SemaphoreType.DMA((2,)),
            ],
            compiler_params=params(20),
            cost_estimate=pl.CostEstimate(
                flops=4 << 30, bytes_accessed=8 << 20, transcendentals=0
            ),
        )(
            sources[first : first + 2],
            down_weight,
            coefs,
            base_down,
            base_out,
            turns[first : first + 2],
            after,
        )

    near = updated(0, hidden)
    hidden = exchange(hidden, "z")
    hidden = pl.pallas_call(
        regroup_kernel,
        in_specs=[VMEM, anywhere],
        out_specs=VMEM,
        out_shape=jax.ShapeDtypeStruct((count + share, wide), BF16),
        compiler_params=params(8),
    )(hidden, near)
    far = updated(2, hidden)
    def shifted(k):
        return lax.ppermute(hidden, "y", [(y, (y + k) % peers_y) for y in range(peers_y)])

    two = shifted(2)
    others = [shifted(1), two, shifted(3)]
    mixed = pl.pallas_call(
        last_kernel,
        in_specs=[VMEM] * 6,
        out_specs=VMEM,
        out_shape=jax.ShapeDtypeStruct((peers_row, 2 * own, feats), BF16),
        compiler_params=params(12),
    )(hidden, *others, near, far)
    mixed = exchange(mixed, PLANE)

    return pl.pallas_call(
        update_kernel,
        in_specs=[VMEM] * 3,
        out_specs=[VMEM] * 2,
        out_shape=[
            jax.ShapeDtypeStruct((own, feats), BF16),
            jax.ShapeDtypeStruct(adam_first.shape, F32),
        ],
        scratch_shapes=[pltpu.VMEM((2, PAD), F32)],
    )(mixed, adam_first, adam_second)


def solution(mesh):
    chips = Mesh(mesh.devices.reshape(4, 2, 8, 4), ("x", "core", "z", "y"))
    tiles = P(("x", "core"), ("z", "y"))
    weights = P(("z", "y"), ("x", "core"))
    placed = (tiles, tiles, weights, weights, tiles, P(), P(), P(), P(), P())
    return jax.shard_map(
        on_device, mesh=chips, in_specs=placed, out_specs=(tiles, P()), check_vma=False
    )
```

```python
import math

import jax
import jax.numpy as jnp
from jax import lax
from jax.experimental import pallas as pl
from jax.experimental.pallas import tpu as pltpu
from jax.sharding import Mesh
from jax.sharding import PartitionSpec as P

D = 8192
FF = 28672
N_COEF = 1000
ADAM_STEP = 3
PAD = 1024
SCALE_UP = 1.0 / math.sqrt(2.0 * D * N_COEF)
SCALE_DOWN = 1.0 / math.sqrt(2.0 * FF * N_COEF)
TWO_PI = 6.283185307179586

F32 = jnp.float32
BF16 = jnp.bfloat16
LOW = 8
MID = 16
SPAN = LOW * MID

PLANE = ("x", "core")
VMEM = pl.BlockSpec(memory_space=pltpu.VMEM)


def params(mib):
    return pltpu.CompilerParams(vmem_limit_bytes=mib << 20)


def waves(index, freq, width, axis):
    phase = index[..., None] * freq % width
    angle = phase.astype(F32) * (TWO_PI / width)
    return jnp.stack([jnp.cos(angle), jnp.sin(angle)], axis=axis)


def phases(freq, first, blocks, width):
    rows = -(-(LOW + MID + blocks) // 8) * 8
    index = jnp.concatenate(
        [
            jnp.arange(LOW, dtype=jnp.int32),
            LOW * jnp.arange(MID, dtype=jnp.int32),
            first + SPAN * jnp.arange(blocks, dtype=jnp.int32),
            jnp.zeros(rows - LOW - MID - blocks, jnp.int32),
        ]
    )
    return waves(index, freq, width, 0)


def span_table(cos, sin):
    low_cos, low_sin = cos[:LOW], sin[:LOW]
    out_cos, out_sin = [], []
    for k in range(MID):
        a, b = cos[LOW + k : LOW + k + 1], sin[LOW + k : LOW + k + 1]
        out_cos.append(a * low_cos - b * low_sin)
        out_sin.append(b * low_cos + a * low_sin)
    return jnp.concatenate(out_cos, axis=0), jnp.concatenate(out_sin, axis=0)


def turned(cos, sin, span_cos, span_sin):
    return cos * span_cos - sin * span_sin, sin * span_cos + cos * span_sin


def against(left, table):
    return lax.dot_general(
        left, table, (((1,), (1,)), ((), ())), preferred_element_type=F32
    )


def matmul(left, right):
    return jnp.dot(left, right, preferred_element_type=F32)


def split(value):
    high = value.astype(BF16)
    return high, (value - high.astype(F32)).astype(BF16)


def spread_kernel(tokens_ref, cotangent_ref, out_ref):
    feats = tokens_ref.shape[1]
    for r in range(out_ref.shape[0]):
        out_ref[r, :, :feats] = tokens_ref[...]
        out_ref[r, :, feats:] = cotangent_ref[...]


def own_table_kernel(base_ref, out_ref):
    for which, sign in ((0, 1.0), (1, -1.0)):
        cos, sin = base_ref[which, 0], base_ref[which, 1]
        span_cos, span_sin = span_table(cos, sin)
        for block in range(out_ref.shape[1] // SPAN):
            at = LOW + MID + block
            c, s = turned(cos[at : at + 1], sin[at : at + 1], span_cos, span_sin)
            rows = slice(block * SPAN, (block + 1) * SPAN)
            out_ref[which, rows, :SPAN] = c.astype(BF16)
            out_ref[which, rows, SPAN:] = (sign * s).astype(BF16)


def late_kernel(rows_ref, cols_ref, coef_ref, after_ref, freq_ref, coef_out):
    del after_ref
    freq_ref[...] = jnp.zeros(freq_ref.shape, jnp.int32)
    coef_out[...] = jnp.zeros(coef_out.shape, F32)
    freq_ref[0:2, :N_COEF] = rows_ref[...]
    freq_ref[2:4, :N_COEF] = cols_ref[...]
    coef_out[:, :N_COEF] = coef_ref[...]


def sum_kernel(*refs):
    total = refs[0][...].astype(F32)
    for ref in refs[1:-1]:
        total += ref[...].astype(F32)
    refs[-1][...] = total.astype(BF16)


def quarter_copies(order_ref, refs, scratch, sems, first):
    wide = scratch[0].shape[2]
    copies = []
    for i in range(scratch[0].shape[0]):
        units = pl.ds(pl.multiple_of(order_ref[first + i] * wide, SPAN), wide)
        places = (refs[0].at[:, units], refs[1].at[:, units], refs[2].at[units, :])
        copies.append(
            [
                pltpu.make_async_copy(place, to.at[i], sems.at[i, k])
                for k, (place, to) in enumerate(zip(places, scratch, strict=True))
            ]
        )
    for three in copies:
        for copy in three:
            copy.start()
    return copies


def quarter_parts(x_ref, scratch, i, copies):
    feats = x_ref.shape[1] // 2
    for copy in copies[i]:
        copy.wait()
    gates, ups, downs = scratch
    tokens, cotangent = x_ref[:, :feats], x_ref[:, feats:]
    return matmul(tokens, gates[i]), matmul(tokens, ups[i]), against(cotangent, downs[i])


def put_halves(low, high, parts):
    half = low.shape[0]
    for at, part in enumerate(parts):
        lanes = slice(at * part.shape[1], (at + 1) * part.shape[1])
        low[:, lanes] = part[:half].astype(BF16)
        high[:, lanes] = part[half:].astype(BF16)


def first_kernel(order_ref, x_ref, gate_ref, up_ref, down_ref, send_a, send_b, *scratch):
    *scratch, sems = scratch
    copies = quarter_copies(order_ref, (gate_ref, up_ref, down_ref), scratch, sems, 0)
    put_halves(send_a, send_b, quarter_parts(x_ref, scratch, 0, copies))


def second_kernel(
    order_ref, x_ref, gate_ref, up_ref, down_ref, after_ref, one_ref, three_ref, *scratch
):
    del after_ref
    *scratch, sems = scratch
    copies = quarter_copies(order_ref, (gate_ref, up_ref, down_ref), scratch, sems, 1)
    half = x_ref.shape[0] // 2
    for i, ref in enumerate((one_ref, three_ref)):
        put_halves(ref.at[:half], ref.at[half:], quarter_parts(x_ref, scratch, i, copies))


def own_kernel(
    order_ref, x_ref, table_ref, gate_ref, up_ref, down_ref, after_ref, proj_ref, own_ref, *scratch
):
    del after_ref
    *scratch, sems = scratch
    copies = quarter_copies(order_ref, (gate_ref, up_ref, down_ref), scratch, sems, 3)
    feats, wide = scratch[0].shape[1:]
    for which in range(2):
        values = x_ref[:, which * feats : (which + 1) * feats]
        lanes = slice(2 * which * SPAN, 2 * (which + 1) * SPAN)
        proj_ref[:, lanes] = matmul(values, table_ref[which]).astype(BF16)
    for at, part in enumerate(quarter_parts(x_ref, scratch, 0, copies)):
        own_ref[:, at * wide : (at + 1) * wide] = part.astype(BF16)


def fold_kernel(one_ref, three_ref, got_a, got_b, proj_ref, send_one, send_three, proj_out):
    proj_out[...] = proj_ref[...]
    half = got_a.shape[0]
    send_one[:half] = one_ref[:half]
    send_one[half:] = (one_ref[half:].astype(F32) + got_b[...].astype(F32)).astype(BF16)
    send_three[:half] = (three_ref[:half].astype(F32) + got_a[...].astype(F32)).astype(BF16)
    send_three[half:] = three_ref[half:]


def close_kernel(own_ref, got_one, got_three, proj_ref, out_ref, proj_out):
    proj_out[...] = proj_ref[...]
    out_ref[...] = (
        own_ref[...].astype(F32) + got_one[...].astype(F32) + got_three[...].astype(F32)
    ).astype(BF16)


def delta_kernel(
    order_ref, down_ref, coef_ref, base_ref, base_out_ref, turn_ref, after_ref, out_ref, *scratch
):
    del after_ref
    left, right, right_turned, down, sems = scratch
    step = pl.program_id(0)
    wide, feats = out_ref.shape
    count = order_ref.shape[0]

    def copy(k):
        units = pl.ds(pl.multiple_of(order_ref[k] * wide, SPAN), wide)
        return pltpu.make_async_copy(down_ref.at[units], down.at[k], sems.at[k])

    @pl.when(step == 0)
    def _():
        for k in range(count):
            copy(k).start()
        for tile in range(PAD // SPAN):
            lanes = slice(tile * SPAN, (tile + 1) * SPAN)
            sines = slice(PAD + tile * SPAN, PAD + (tile + 1) * SPAN)
            cos, sin = base_ref[0, :, lanes], base_ref[1, :, lanes]
            span_cos, span_sin = span_table(cos, sin)
            for block in range(wide // SPAN):
                at = LOW + MID + block
                c, s = turned(cos[at : at + 1], sin[at : at + 1], span_cos, span_sin)
                units = slice(block * SPAN, (block + 1) * SPAN)
                left[units, lanes] = c.astype(BF16)
                left[units, sines] = s.astype(BF16)
            coef = coef_ref[1:2, lanes] * SCALE_DOWN
            cos, sin = base_out_ref[0, :, lanes], base_out_ref[1, :, lanes]
            span_cos, span_sin = span_table(cos, sin)
            for block in range(feats // SPAN):
                at = LOW + MID + block
                c, s = turned(cos[at : at + 1], sin[at : at + 1], span_cos, span_sin)
                rows = slice(block * SPAN, (block + 1) * SPAN)
                right[0, rows, lanes] = c * coef
                right[1, rows, lanes] = -s * coef

    for tile in range(PAD // SPAN):
        lanes = slice(tile * SPAN, (tile + 1) * SPAN)
        sines = slice(PAD + tile * SPAN, PAD + (tile + 1) * SPAN)
        cos, sin = turn_ref[0, 0:1, lanes], turn_ref[0, 1:2, lanes]
        for rows in (slice(i, i + 64) for i in range(0, feats, 64)):
            c, s = right[0, rows, lanes], right[1, rows, lanes]
            right_turned[rows, lanes] = (cos * c + sin * s).astype(BF16)
            right_turned[rows, sines] = (cos * s - sin * c).astype(BF16)
    delta = against(left[...], right_turned[...])
    copy(step).wait()
    out_ref[...] = (down[step].astype(F32) + delta).astype(BF16)


def summed(ref, first, last):
    total = ref[0, :, first:last].astype(F32)
    for z in range(1, ref.shape[0]):
        total += ref[z, :, first:last].astype(F32)
    return total


def twice(ref, row):
    return jnp.concatenate([ref[row : row + 1], ref[row : row + 1]], axis=1)


def middle_kernel(
    source_ref, sums_ref, proj_ref, coef_ref, base_ref, out_ref, span_ref
):
    rows, lanes_sent = out_ref.shape[1:]
    wide = lanes_sent - SPAN
    blocks = wide // SPAN
    for which in range(2):
        for tile in range(PAD // SPAN):
            lanes = slice(tile * SPAN, (tile + 1) * SPAN)
            c, s = span_table(base_ref[which, 0, :, lanes], base_ref[which, 1, :, lanes])
            span_ref[which, :, lanes] = c.astype(BF16)
            span_ref[which, :, PAD + tile * SPAN : PAD + (tile + 1) * SPAN] = s.astype(BF16)

    def phase(which, block):
        at = slice(LOW + MID + block, LOW + MID + block + 1)
        return base_ref[which, 0, at, :], base_ref[which, 1, at, :]

    def spread(weighted, which, sign):
        by_cos, by_sin = weighted[:, :PAD], sign * weighted[:, PAD:]
        pieces = []
        for block in range(blocks):
            cos, sin = phase(which, block)
            pieces.append(
                jnp.concatenate(
                    [by_cos * cos + by_sin * sin, by_sin * cos - by_cos * sin], axis=1
                ).astype(BF16)
            )
        value = against(jnp.concatenate(pieces, axis=0), span_ref[which])
        return jnp.concatenate(
            [value[block * rows : (block + 1) * rows] for block in range(blocks)], axis=1
        )

    def collect(value, which, sign):
        stacked = jnp.concatenate(
            [value[:, block * SPAN : (block + 1) * SPAN] for block in range(blocks)], axis=0
        )
        found = matmul(stacked, span_ref[which])
        by_cos = jnp.zeros((rows, PAD), F32)
        by_sin = jnp.zeros((rows, PAD), F32)
        for block in range(blocks):
            cos, sin = phase(which, block)
            x = found[block * rows : (block + 1) * rows, :PAD]
            y = found[block * rows : (block + 1) * rows, PAD:]
            by_cos += cos * x - sin * y
            by_sin += sin * x + cos * y
        return by_cos, sign * by_sin

    def kind(k):
        lanes = slice(k * SPAN, (k + 1) * SPAN)
        return [
            proj_ref[source_ref[x], source_ref[4 + c], :, lanes].astype(F32)
            for x in range(proj_ref.shape[0])
            for c in range(proj_ref.shape[1])
        ]

    proj_up = jnp.concatenate(kind(0) + kind(1), axis=1)
    back_down = jnp.concatenate(kind(2) + kind(3), axis=1)
    gate = summed(sums_ref, 0, wide)
    up = summed(sums_ref, wide, 2 * wide) + spread(proj_up * (twice(coef_ref, 0) * SCALE_UP), 0, -1.0)
    dhidden = summed(sums_ref, 2 * wide, 3 * wide) + spread(back_down * (twice(coef_ref, 1) * SCALE_DOWN), 1, 1.0)
    activated = (gate / (1.0 + jnp.exp(-gate))).astype(BF16).astype(F32)
    hidden = (activated * up).astype(BF16)
    dup = (dhidden * activated).astype(BF16)
    up_cos, up_sin = collect(dup, 0, -1.0)
    down_cos, down_sin = collect(hidden, 1, 1.0)

    def over_tokens(value):
        return jnp.sum(value, axis=0, keepdims=True)

    grad_up = SCALE_UP * over_tokens(proj_up[:, :PAD] * up_cos + proj_up[:, PAD:] * up_sin)
    grad_down = SCALE_DOWN * over_tokens(
        down_cos * back_down[:, :PAD] + down_sin * back_down[:, PAD:]
    )
    grads = jnp.concatenate(
        [g[:, k * SPAN : (k + 1) * SPAN] for g in (grad_up, grad_down) for k in range(PAD // SPAN)],
        axis=0,
    ).astype(BF16)
    for c in range(out_ref.shape[0]):
        out_ref[c, :, :wide] = hidden
        out_ref[c, :, wide:] = grads


def regroup_kernel(in_ref, after_ref, out_ref):
    del after_ref
    peers, rows, _ = in_ref.shape
    wide = out_ref.shape[1]
    grads = jnp.zeros((rows, SPAN), F32)
    for z in range(peers):
        out_ref[z * rows : (z + 1) * rows, :] = in_ref[z, :, :wide]
        grads += in_ref[z, :, wide:].astype(F32)
    high, low = split(grads)
    out_ref[peers * rows :, :SPAN] = high
    out_ref[peers * rows :, SPAN : 2 * SPAN] = low
    out_ref[peers * rows :, 2 * SPAN :] = jnp.zeros((rows, wide - 2 * SPAN), BF16)


def last_kernel(own_ref, one_ref, two_ref, three_ref, near_ref, far_ref, out_ref):
    peers, rows, feats = out_ref.shape
    rows //= 2
    wide = own_ref.shape[1]
    count = peers * rows
    total = jnp.zeros((count, feats), F32)
    grads = jnp.zeros((own_ref.shape[0] - count, SPAN), F32)
    for k, ref in enumerate((own_ref, one_ref, two_ref, three_ref)):
        weight_ref = (near_ref, far_ref)[k // 2]
        units = slice(k % 2 * wide, (k % 2 + 1) * wide)
        total += matmul(ref[:count, :], weight_ref[units, :])
        grads += ref[count:, :SPAN].astype(F32) + ref[count:, SPAN : 2 * SPAN].astype(F32)
    high, low = split(grads)
    for r in range(peers):
        out_ref[r, :rows, :] = total[r * rows : (r + 1) * rows, :].astype(BF16)
        out_ref[r, rows:, :SPAN] = high
        out_ref[r, rows:, SPAN:] = low


def update_kernel(in_ref, first_ref, second_ref, mixed_ref, step_ref, scratch):
    peers, rows, _ = in_ref.shape
    rows //= 2
    mixed = jnp.zeros(mixed_ref.shape, F32)
    pieces = jnp.zeros((rows, SPAN), F32)
    for r in range(peers):
        mixed += in_ref[r, :rows, :].astype(F32)
        pieces += in_ref[r, rows:, :SPAN].astype(F32)
        pieces += in_ref[r, rows:, SPAN:].astype(F32)
    mixed_ref[...] = mixed.astype(BF16)
    per = PAD // SPAN
    for k in range(rows):
        at = k % per
        scratch[k // per : k // per + 1, at * SPAN : (at + 1) * SPAN] = pieces[k : k + 1]
    grads = scratch[:, :N_COEF]
    squares = jnp.sum(jnp.sum(grads * grads, axis=1, keepdims=True), axis=0, keepdims=True)
    norm_value = jnp.sqrt(squares)
    clipped = grads * jnp.minimum(1.0, 1.0 / (norm_value + 1e-06))
    first = 0.9 * first_ref[...] + 0.1 * clipped
    second = 0.999 * second_ref[...] + 0.001 * clipped * clipped
    step_ref[...] = (
        first / (1.0 - 0.9**ADAM_STEP) / (jnp.sqrt(second / (1.0 - 0.999**ADAM_STEP)) + 1e-08)
    )


def on_device(
    tokens,
    cotangent,
    gate_weight,
    up_weight,
    down_weight,
    coefficients,
    spectral_rows,
    spectral_cols,
    adam_first,
    adam_second,
):
    peers_row = lax.axis_size(PLANE)
    peers_z = lax.axis_size("z")
    peers_y = lax.axis_size("y")
    row_index = lax.axis_index(PLANE)
    z_index = lax.axis_index("z")
    y_index = lax.axis_index("y")
    own, feats = tokens.shape
    units = gate_weight.shape[1]
    wide = units // peers_y
    count = own * peers_row
    feat_first = (z_index * peers_y + y_index) * feats
    unit_first = row_index * units

    def exchange(value, axes):
        return lax.all_to_all(value, axes, 0, 0, tiled=True)

    def padded(values):
        return jnp.pad(values, (0, PAD - N_COEF))

    lanes = row_index * SPAN
    own_left = lax.dynamic_slice_in_dim(padded(spectral_rows[0]), lanes, SPAN)
    own_right = lax.dynamic_slice_in_dim(padded(spectral_cols[1]), lanes, SPAN)
    base_own = jnp.stack(
        [
            phases(own_left, feat_first, feats // SPAN, D),
            phases(own_right, feat_first, feats // SPAN, D),
        ]
    )

    both = pl.pallas_call(
        spread_kernel,
        in_specs=[VMEM] * 2,
        out_specs=VMEM,
        out_shape=jax.ShapeDtypeStruct((peers_row, own, 2 * feats), BF16),
    )(tokens, cotangent)
    both = exchange(both, PLANE).reshape(count, 2 * feats)

    share = count // peers_z
    half = count // 2
    block = 3 * wide
    smem = pl.BlockSpec(memory_space=pltpu.SMEM)
    hbm = pl.BlockSpec(memory_space=pltpu.HBM)
    anywhere = pl.BlockSpec(memory_space=pl.ANY)
    order = y_index ^ jnp.array([2, 1, 3, 0], jnp.int32)

    def full(shape):
        return pl.BlockSpec(shape, lambda i: (0,) * len(shape))

    table = pl.pallas_call(
        own_table_kernel,
        in_specs=[VMEM],
        out_specs=VMEM,
        out_shape=jax.ShapeDtypeStruct((2, feats, 2 * SPAN), BF16),
        compiler_params=params(8),
    )(base_own)
    def scratch(quarters):
        return [
            pltpu.VMEM((quarters, feats, wide), BF16),
            pltpu.VMEM((quarters, feats, wide), BF16),
            pltpu.VMEM((quarters, wide, feats), BF16),
            pltpu.SemaphoreType.DMA((quarters, 3)),
        ]

    piece = jax.ShapeDtypeStruct((half, block), BF16)
    def swap(value, mask):
        return lax.ppermute(value, "y", [(y, y ^ mask) for y in range(peers_y)])

    early_a, early_b = pl.pallas_call(
        first_kernel,
        in_specs=[smem, VMEM, hbm, hbm, hbm],
        out_specs=[VMEM] * 2,
        out_shape=[piece] * 2,
        scratch_shapes=scratch(1),
        compiler_params=params(52),
    )(order, both, gate_weight, up_weight, down_weight)
    got_early_a, got_early_b = swap(early_a, 1), swap(early_b, 3)
    one, three = pl.pallas_call(
        second_kernel,
        in_specs=[smem, VMEM, hbm, hbm, hbm, VMEM],
        out_specs=[VMEM] * 2,
        out_shape=[jax.ShapeDtypeStruct((count, block), BF16)] * 2,
        scratch_shapes=scratch(2),
        compiler_params=params(52),
    )(order, both, gate_weight, up_weight, down_weight, early_a)
    proj, mine = pl.pallas_call(
        own_kernel,
        in_specs=[smem, VMEM, VMEM, hbm, hbm, hbm, VMEM],
        out_specs=[VMEM] * 2,
        out_shape=[
            jax.ShapeDtypeStruct((count, peers_y * SPAN), BF16),
            jax.ShapeDtypeStruct((count, block), BF16),
        ],
        scratch_shapes=scratch(1),
        compiler_params=params(52),
    )(order, both, table, gate_weight, up_weight, down_weight, one)

    freq, coefs = pl.pallas_call(
        late_kernel,
        in_specs=[VMEM] * 4,
        out_specs=[VMEM] * 2,
        out_shape=[
            jax.ShapeDtypeStruct((4, PAD), jnp.int32),
            jax.ShapeDtypeStruct((2, PAD), F32),
        ],
    )(spectral_rows, spectral_cols, coefficients, one)
    tile_first = unit_first + y_index * wide
    base_up = phases(freq[2], tile_first, wide // SPAN, FF)
    base_down = phases(freq[1], tile_first, wide // SPAN, FF)
    base_out = phases(freq[3], feat_first, feats // SPAN, D)
    sources = (y_index - jnp.arange(peers_y, dtype=jnp.int32)) & 3
    turns = waves(((sources - y_index) * wide)[:, None], freq[1], FF, 1)
    turns = turns.reshape(peers_y, 2, PAD)

    def added(values):
        return pl.pallas_call(
            sum_kernel,
            in_specs=[VMEM] * len(values),
            out_specs=VMEM,
            out_shape=jax.ShapeDtypeStruct(values[0].shape, BF16),
            compiler_params=params(8),
        )(*values)

    def turn(value, axis, peers, k):
        return lax.ppermute(value, axis, [(i, (i + k) % peers) for i in range(peers)])

    one, three, proj = pl.pallas_call(
        fold_kernel,
        in_specs=[VMEM] * 5,
        out_specs=[VMEM] * 3,
        out_shape=[jax.ShapeDtypeStruct((count, block), BF16)] * 2
        + [jax.ShapeDtypeStruct(proj.shape, BF16)],
        compiler_params=params(8),
    )(one, three, got_early_a, got_early_b, proj)
    got_one, got_three = swap(one, 1), swap(three, 3)
    proj = exchange(proj.reshape(peers_z, share, peers_y * SPAN), "z")
    proj = jnp.sum(proj.astype(F32), axis=0).astype(BF16)
    sums, proj = pl.pallas_call(
        close_kernel,
        in_specs=[VMEM] * 4,
        out_specs=[VMEM] * 2,
        out_shape=[
            jax.ShapeDtypeStruct((count, block), BF16),
            jax.ShapeDtypeStruct(proj.shape, BF16),
        ],
        compiler_params=params(8),
    )(mine, got_one, got_three, proj)
    proj = added([proj] + [turn(proj, "y", peers_y, k) for k in (1, 2, 3)])
    proj = jnp.stack([proj, lax.ppermute(proj, "core", [(0, 1), (1, 0)])])
    proj = jnp.stack([proj] + [turn(proj, "x", 4, k) for k in (1, 2, 3)])
    chip = (lax.axis_index("x") - jnp.arange(4, dtype=jnp.int32)) & 3
    core = lax.axis_index("core") ^ jnp.arange(2, dtype=jnp.int32)
    source = jnp.concatenate([chip, core])
    sums = exchange(sums.reshape(peers_z, share, block), "z")

    hidden = pl.pallas_call(
        middle_kernel,
        in_specs=[smem] + [VMEM] * 4,
        out_specs=VMEM,
        out_shape=jax.ShapeDtypeStruct((peers_z, share, wide + SPAN), BF16),
        scratch_shapes=[pltpu.VMEM((2, SPAN, 2 * PAD), BF16)],
        compiler_params=params(12),
    )(source, sums, proj, coefs, jnp.stack([base_up, base_down]))
    def updated(first, after):
        return pl.pallas_call(
            delta_kernel,
            grid=(2,),
            in_specs=[
                smem,
                hbm,
                full(coefs.shape),
                full(base_down.shape),
                full(base_out.shape),
                pl.BlockSpec((1,) + turns.shape[1:], lambda i: (i, 0, 0)),
                anywhere,
            ],
            out_specs=pl.BlockSpec((wide, feats), lambda i: (i, 0)),
            out_shape=jax.ShapeDtypeStruct((2 * wide, feats), BF16),
            scratch_shapes=[
                pltpu.VMEM((wide, 2 * PAD), BF16),
                pltpu.VMEM((2, feats, PAD), F32),
                pltpu.VMEM((feats, 2 * PAD), BF16),
                pltpu.VMEM((2, wide, feats), BF16),
                pltpu.SemaphoreType.DMA((2,)),
            ],
            compiler_params=params(20),
            cost_estimate=pl.CostEstimate(
                flops=4 << 30, bytes_accessed=8 << 20, transcendentals=0
            ),
        )(
            sources[first : first + 2],
            down_weight,
            coefs,
            base_down,
            base_out,
            turns[first : first + 2],
            after,
        )

    near = updated(0, hidden)
    hidden = exchange(hidden, "z")
    hidden = pl.pallas_call(
        regroup_kernel,
        in_specs=[VMEM, anywhere],
        out_specs=VMEM,
        out_shape=jax.ShapeDtypeStruct((count + share, wide), BF16),
        compiler_params=params(8),
    )(hidden, near)
    far = updated(2, hidden)
    def shifted(k):
        return lax.ppermute(hidden, "y", [(y, (y + k) % peers_y) for y in range(peers_y)])

    two = shifted(2)
    others = [shifted(1), two, shifted(3)]
    mixed = pl.pallas_call(
        last_kernel,
        in_specs=[VMEM] * 6,
        out_specs=VMEM,
        out_shape=jax.ShapeDtypeStruct((peers_row, 2 * own, feats), BF16),
        compiler_params=params(12),
    )(hidden, *others, near, far)
    mixed = exchange(mixed, PLANE)

    return pl.pallas_call(
        update_kernel,
        in_specs=[VMEM] * 3,
        out_specs=[VMEM] * 2,
        out_shape=[
            jax.ShapeDtypeStruct((own, feats), BF16),
            jax.ShapeDtypeStruct(adam_first.shape, F32),
        ],
        scratch_shapes=[pltpu.VMEM((2, PAD), F32)],
    )(mixed, adam_first, adam_second)


def solution(mesh):
    chips = Mesh(mesh.devices.reshape(4, 2, 8, 4), ("x", "core", "z", "y"))
    tiles = P(("x", "core"), ("z", "y"))
    weights = P(("z", "y"), ("x", "core"))
    placed = (tiles, tiles, weights, weights, tiles, P(), P(), P(), P(), P())
    return jax.shard_map(
        on_device, mesh=chips, in_specs=placed, out_specs=(tiles, P()), check_vma=False
    )
```

```python
import math

import jax
import jax.numpy as jnp
from jax import lax
from jax.experimental import pallas as pl
from jax.experimental.pallas import tpu as pltpu
from jax.sharding import Mesh
from jax.sharding import PartitionSpec as P

D = 8192
FF = 28672
N_COEF = 1000
ADAM_STEP = 3
PAD = 1024
SCALE_UP = 1.0 / math.sqrt(2.0 * D * N_COEF)
SCALE_DOWN = 1.0 / math.sqrt(2.0 * FF * N_COEF)
TWO_PI = 6.283185307179586

F32 = jnp.float32
BF16 = jnp.bfloat16
LOW = 8
MID = 16
SPAN = LOW * MID

PLANE = ("x", "core")
VMEM = pl.BlockSpec(memory_space=pltpu.VMEM)


def params(mib):
    return pltpu.CompilerParams(vmem_limit_bytes=mib << 20)


def waves(index, freq, width, axis):
    phase = index[..., None] * freq % width
    angle = phase.astype(F32) * (TWO_PI / width)
    return jnp.stack([jnp.cos(angle), jnp.sin(angle)], axis=axis)


def phases(freq, first, blocks, width):
    rows = -(-(LOW + MID + blocks) // 8) * 8
    index = jnp.concatenate(
        [
            jnp.arange(LOW, dtype=jnp.int32),
            LOW * jnp.arange(MID, dtype=jnp.int32),
            first + SPAN * jnp.arange(blocks, dtype=jnp.int32),
            jnp.zeros(rows - LOW - MID - blocks, jnp.int32),
        ]
    )
    return waves(index, freq, width, 0)


def span_table(cos, sin):
    low_cos, low_sin = cos[:LOW], sin[:LOW]
    out_cos, out_sin = [], []
    for k in range(MID):
        a, b = cos[LOW + k : LOW + k + 1], sin[LOW + k : LOW + k + 1]
        out_cos.append(a * low_cos - b * low_sin)
        out_sin.append(b * low_cos + a * low_sin)
    return jnp.concatenate(out_cos, axis=0), jnp.concatenate(out_sin, axis=0)


def turned(cos, sin, span_cos, span_sin):
    return cos * span_cos - sin * span_sin, sin * span_cos + cos * span_sin


def against(left, table):
    return lax.dot_general(
        left, table, (((1,), (1,)), ((), ())), preferred_element_type=F32
    )


def matmul(left, right):
    return jnp.dot(left, right, preferred_element_type=F32)


def split(value):
    high = value.astype(BF16)
    return high, (value - high.astype(F32)).astype(BF16)


def spread_kernel(tokens_ref, cotangent_ref, out_ref):
    feats = tokens_ref.shape[1]
    for r in range(out_ref.shape[0]):
        out_ref[r, :, :feats] = tokens_ref[...]
        out_ref[r, :, feats:] = cotangent_ref[...]


def own_table_kernel(base_ref, out_ref):
    for which, sign in ((0, 1.0), (1, -1.0)):
        cos, sin = base_ref[which, 0], base_ref[which, 1]
        span_cos, span_sin = span_table(cos, sin)
        for block in range(out_ref.shape[1] // SPAN):
            at = LOW + MID + block
            c, s = turned(cos[at : at + 1], sin[at : at + 1], span_cos, span_sin)
            rows = slice(block * SPAN, (block + 1) * SPAN)
            out_ref[which, rows, :SPAN] = c.astype(BF16)
            out_ref[which, rows, SPAN:] = (sign * s).astype(BF16)


def late_kernel(rows_ref, cols_ref, coef_ref, after_ref, freq_ref, coef_out):
    del after_ref
    freq_ref[...] = jnp.zeros(freq_ref.shape, jnp.int32)
    coef_out[...] = jnp.zeros(coef_out.shape, F32)
    freq_ref[0:2, :N_COEF] = rows_ref[...]
    freq_ref[2:4, :N_COEF] = cols_ref[...]
    coef_out[:, :N_COEF] = coef_ref[...]


def sum_kernel(*refs):
    total = refs[0][...].astype(F32)
    for ref in refs[1:-1]:
        total += ref[...].astype(F32)
    refs[-1][...] = total.astype(BF16)


def quarter_copies(order_ref, refs, scratch, sems, first):
    wide = scratch[0].shape[2]
    copies = []
    for i in range(scratch[0].shape[0]):
        units = pl.ds(pl.multiple_of(order_ref[first + i] * wide, SPAN), wide)
        places = (refs[0].at[:, units], refs[1].at[:, units], refs[2].at[units, :])
        copies.append(
            [
                pltpu.make_async_copy(place, to.at[i], sems.at[i, k])
                for k, (place, to) in enumerate(zip(places, scratch, strict=True))
            ]
        )
    for three in copies:
        for copy in three:
            copy.start()
    return copies


def quarter_parts(x_ref, scratch, i, copies):
    feats = x_ref.shape[1] // 2
    for copy in copies[i]:
        copy.wait()
    gates, ups, downs = scratch
    tokens, cotangent = x_ref[:, :feats], x_ref[:, feats:]
    return matmul(tokens, gates[i]), matmul(tokens, ups[i]), against(cotangent, downs[i])


def put_halves(low, high, parts):
    half = low.shape[0]
    for at, part in enumerate(parts):
        lanes = slice(at * part.shape[1], (at + 1) * part.shape[1])
        low[:, lanes] = part[:half].astype(BF16)
        high[:, lanes] = part[half:].astype(BF16)


def first_kernel(order_ref, x_ref, gate_ref, up_ref, down_ref, send_a, send_b, *scratch):
    *scratch, sems = scratch
    copies = quarter_copies(order_ref, (gate_ref, up_ref, down_ref), scratch, sems, 0)
    put_halves(send_a, send_b, quarter_parts(x_ref, scratch, 0, copies))


def second_kernel(
    order_ref, x_ref, gate_ref, up_ref, down_ref, after_ref, one_ref, three_ref, *scratch
):
    del after_ref
    *scratch, sems = scratch
    copies = quarter_copies(order_ref, (gate_ref, up_ref, down_ref), scratch, sems, 1)
    half = x_ref.shape[0] // 2
    for i, ref in enumerate((one_ref, three_ref)):
        put_halves(ref.at[:half], ref.at[half:], quarter_parts(x_ref, scratch, i, copies))


def own_kernel(
    order_ref, x_ref, table_ref, gate_ref, up_ref, down_ref, after_ref, proj_ref, own_ref, *scratch
):
    del after_ref
    *scratch, sems = scratch
    copies = quarter_copies(order_ref, (gate_ref, up_ref, down_ref), scratch, sems, 3)
    feats, wide = scratch[0].shape[1:]
    for which in range(2):
        values = x_ref[:, which * feats : (which + 1) * feats]
        lanes = slice(2 * which * SPAN, 2 * (which + 1) * SPAN)
        proj_ref[:, lanes] = matmul(values, table_ref[which]).astype(BF16)
    for at, part in enumerate(quarter_parts(x_ref, scratch, 0, copies)):
        own_ref[:, at * wide : (at + 1) * wide] = part.astype(BF16)


def fold_kernel(one_ref, three_ref, got_a, got_b, proj_ref, send_one, send_three, proj_out):
    proj_out[...] = proj_ref[...]
    half = got_a.shape[0]
    send_one[:half] = one_ref[:half]
    send_one[half:] = (one_ref[half:].astype(F32) + got_b[...].astype(F32)).astype(BF16)
    send_three[:half] = (three_ref[:half].astype(F32) + got_a[...].astype(F32)).astype(BF16)
    send_three[half:] = three_ref[half:]


def close_kernel(own_ref, got_one, got_three, proj_ref, out_ref, proj_out):
    proj_out[...] = proj_ref[...]
    out_ref[...] = (
        own_ref[...].astype(F32) + got_one[...].astype(F32) + got_three[...].astype(F32)
    ).astype(BF16)


def delta_kernel(
    order_ref, down_ref, coef_ref, base_ref, base_out_ref, turn_ref, after_ref, out_ref, *scratch
):
    del after_ref
    left, right, right_turned, down, sems = scratch
    step = pl.program_id(0)
    wide, feats = out_ref.shape
    count = order_ref.shape[0]

    def copy(k):
        units = pl.ds(pl.multiple_of(order_ref[k] * wide, SPAN), wide)
        return pltpu.make_async_copy(down_ref.at[units], down.at[k], sems.at[k])

    @pl.when(step == 0)
    def _():
        for k in range(count):
            copy(k).start()
        for tile in range(PAD // SPAN):
            lanes = slice(tile * SPAN, (tile + 1) * SPAN)
            sines = slice(PAD + tile * SPAN, PAD + (tile + 1) * SPAN)
            cos, sin = base_ref[0, :, lanes], base_ref[1, :, lanes]
            span_cos, span_sin = span_table(cos, sin)
            for block in range(wide // SPAN):
                at = LOW + MID + block
                c, s = turned(cos[at : at + 1], sin[at : at + 1], span_cos, span_sin)
                units = slice(block * SPAN, (block + 1) * SPAN)
                left[units, lanes] = c.astype(BF16)
                left[units, sines] = s.astype(BF16)
            coef = coef_ref[1:2, lanes] * SCALE_DOWN
            cos, sin = base_out_ref[0, :, lanes], base_out_ref[1, :, lanes]
            span_cos, span_sin = span_table(cos, sin)
            for block in range(feats // SPAN):
                at = LOW + MID + block
                c, s = turned(cos[at : at + 1], sin[at : at + 1], span_cos, span_sin)
                rows = slice(block * SPAN, (block + 1) * SPAN)
                right[0, rows, lanes] = c * coef
                right[1, rows, lanes] = -s * coef

    for tile in range(PAD // SPAN):
        lanes = slice(tile * SPAN, (tile + 1) * SPAN)
        sines = slice(PAD + tile * SPAN, PAD + (tile + 1) * SPAN)
        cos, sin = turn_ref[0, 0:1, lanes], turn_ref[0, 1:2, lanes]
        for rows in (slice(i, i + 64) for i in range(0, feats, 64)):
            c, s = right[0, rows, lanes], right[1, rows, lanes]
            right_turned[rows, lanes] = (cos * c + sin * s).astype(BF16)
            right_turned[rows, sines] = (cos * s - sin * c).astype(BF16)
    delta = against(left[...], right_turned[...])
    copy(step).wait()
    out_ref[...] = (down[step].astype(F32) + delta).astype(BF16)


def summed(ref, first, last):
    total = ref[0, :, first:last].astype(F32)
    for z in range(1, ref.shape[0]):
        total += ref[z, :, first:last].astype(F32)
    return total


def twice(ref, row):
    return jnp.concatenate([ref[row : row + 1], ref[row : row + 1]], axis=1)


def middle_kernel(
    source_ref, sums_ref, proj_ref, coef_ref, base_ref, out_ref, span_ref
):
    rows, lanes_sent = out_ref.shape[1:]
    wide = lanes_sent - SPAN
    blocks = wide // SPAN
    for which in range(2):
        for tile in range(PAD // SPAN):
            lanes = slice(tile * SPAN, (tile + 1) * SPAN)
            c, s = span_table(base_ref[which, 0, :, lanes], base_ref[which, 1, :, lanes])
            span_ref[which, :, lanes] = c.astype(BF16)
            span_ref[which, :, PAD + tile * SPAN : PAD + (tile + 1) * SPAN] = s.astype(BF16)

    def phase(which, block):
        at = slice(LOW + MID + block, LOW + MID + block + 1)
        return base_ref[which, 0, at, :], base_ref[which, 1, at, :]

    def spread(weighted, which, sign):
        by_cos, by_sin = weighted[:, :PAD], sign * weighted[:, PAD:]
        pieces = []
        for block in range(blocks):
            cos, sin = phase(which, block)
            pieces.append(
                jnp.concatenate(
                    [by_cos * cos + by_sin * sin, by_sin * cos - by_cos * sin], axis=1
                ).astype(BF16)
            )
        value = against(jnp.concatenate(pieces, axis=0), span_ref[which])
        return jnp.concatenate(
            [value[block * rows : (block + 1) * rows] for block in range(blocks)], axis=1
        )

    def collect(value, which, sign):
        stacked = jnp.concatenate(
            [value[:, block * SPAN : (block + 1) * SPAN] for block in range(blocks)], axis=0
        )
        found = matmul(stacked, span_ref[which])
        by_cos = jnp.zeros((rows, PAD), F32)
        by_sin = jnp.zeros((rows, PAD), F32)
        for block in range(blocks):
            cos, sin = phase(which, block)
            x = found[block * rows : (block + 1) * rows, :PAD]
            y = found[block * rows : (block + 1) * rows, PAD:]
            by_cos += cos * x - sin * y
            by_sin += sin * x + cos * y
        return by_cos, sign * by_sin

    def kind(k):
        lanes = slice(k * SPAN, (k + 1) * SPAN)
        return [
            proj_ref[source_ref[x], source_ref[4 + c], :, lanes].astype(F32)
            for x in range(proj_ref.shape[0])
            for c in range(proj_ref.shape[1])
        ]

    proj_up = jnp.concatenate(kind(0) + kind(1), axis=1)
    back_down = jnp.concatenate(kind(2) + kind(3), axis=1)
    gate = summed(sums_ref, 0, wide)
    up = summed(sums_ref, wide, 2 * wide) + spread(proj_up * (twice(coef_ref, 0) * SCALE_UP), 0, -1.0)
    dhidden = summed(sums_ref, 2 * wide, 3 * wide) + spread(back_down * (twice(coef_ref, 1) * SCALE_DOWN), 1, 1.0)
    activated = (gate / (1.0 + jnp.exp(-gate))).astype(BF16).astype(F32)
    hidden = (activated * up).astype(BF16)
    dup = (dhidden * activated).astype(BF16)
    up_cos, up_sin = collect(dup, 0, -1.0)
    down_cos, down_sin = collect(hidden, 1, 1.0)

    def over_tokens(value):
        return jnp.sum(value, axis=0, keepdims=True)

    grad_up = SCALE_UP * over_tokens(proj_up[:, :PAD] * up_cos + proj_up[:, PAD:] * up_sin)
    grad_down = SCALE_DOWN * over_tokens(
        down_cos * back_down[:, :PAD] + down_sin * back_down[:, PAD:]
    )
    grads = jnp.concatenate(
        [g[:, k * SPAN : (k + 1) * SPAN] for g in (grad_up, grad_down) for k in range(PAD // SPAN)],
        axis=0,
    ).astype(BF16)
    for c in range(out_ref.shape[0]):
        out_ref[c, :, :wide] = hidden
        out_ref[c, :, wide:] = grads


def regroup_kernel(in_ref, after_ref, out_ref):
    del after_ref
    peers, rows, _ = in_ref.shape
    wide = out_ref.shape[1]
    grads = jnp.zeros((rows, SPAN), F32)
    for z in range(peers):
        out_ref[z * rows : (z + 1) * rows, :] = in_ref[z, :, :wide]
        grads += in_ref[z, :, wide:].astype(F32)
    high, low = split(grads)
    out_ref[peers * rows :, :SPAN] = high
    out_ref[peers * rows :, SPAN : 2 * SPAN] = low
    out_ref[peers * rows :, 2 * SPAN :] = jnp.zeros((rows, wide - 2 * SPAN), BF16)


def last_kernel(own_ref, one_ref, two_ref, three_ref, near_ref, far_ref, out_ref):
    peers, rows, feats = out_ref.shape
    rows //= 2
    wide = own_ref.shape[1]
    count = peers * rows
    total = jnp.zeros((count, feats), F32)
    grads = jnp.zeros((own_ref.shape[0] - count, SPAN), F32)
    for k, ref in enumerate((own_ref, one_ref, two_ref, three_ref)):
        weight_ref = (near_ref, far_ref)[k // 2]
        units = slice(k % 2 * wide, (k % 2 + 1) * wide)
        total += matmul(ref[:count, :], weight_ref[units, :])
        grads += ref[count:, :SPAN].astype(F32) + ref[count:, SPAN : 2 * SPAN].astype(F32)
    high, low = split(grads)
    for r in range(peers):
        out_ref[r, :rows, :] = total[r * rows : (r + 1) * rows, :].astype(BF16)
        out_ref[r, rows:, :SPAN] = high
        out_ref[r, rows:, SPAN:] = low


def update_kernel(in_ref, first_ref, second_ref, mixed_ref, step_ref, scratch):
    peers, rows, _ = in_ref.shape
    rows //= 2
    mixed = jnp.zeros(mixed_ref.shape, F32)
    pieces = jnp.zeros((rows, SPAN), F32)
    for r in range(peers):
        mixed += in_ref[r, :rows, :].astype(F32)
        pieces += in_ref[r, rows:, :SPAN].astype(F32)
        pieces += in_ref[r, rows:, SPAN:].astype(F32)
    mixed_ref[...] = mixed.astype(BF16)
    per = PAD // SPAN
    for k in range(rows):
        at = k % per
        scratch[k // per : k // per + 1, at * SPAN : (at + 1) * SPAN] = pieces[k : k + 1]
    grads = scratch[:, :N_COEF]
    squares = jnp.sum(jnp.sum(grads * grads, axis=1, keepdims=True), axis=0, keepdims=True)
    norm_value = jnp.sqrt(squares)
    clipped = grads * jnp.minimum(1.0, 1.0 / (norm_value + 1e-06))
    first = 0.9 * first_ref[...] + 0.1 * clipped
    second = 0.999 * second_ref[...] + 0.001 * clipped * clipped
    step_ref[...] = (
        first / (1.0 - 0.9**ADAM_STEP) / (jnp.sqrt(second / (1.0 - 0.999**ADAM_STEP)) + 1e-08)
    )


def on_device(
    tokens,
    cotangent,
    gate_weight,
    up_weight,
    down_weight,
    coefficients,
    spectral_rows,
    spectral_cols,
    adam_first,
    adam_second,
):
    peers_row = lax.axis_size(PLANE)
    peers_z = lax.axis_size("z")
    peers_y = lax.axis_size("y")
    row_index = lax.axis_index(PLANE)
    z_index = lax.axis_index("z")
    y_index = lax.axis_index("y")
    own, feats = tokens.shape
    units = gate_weight.shape[1]
    wide = units // peers_y
    count = own * peers_row
    feat_first = (z_index * peers_y + y_index) * feats
    unit_first = row_index * units

    def exchange(value, axes):
        return lax.all_to_all(value, axes, 0, 0, tiled=True)

    def padded(values):
        return jnp.pad(values, (0, PAD - N_COEF))

    lanes = row_index * SPAN
    own_left = lax.dynamic_slice_in_dim(padded(spectral_rows[0]), lanes, SPAN)
    own_right = lax.dynamic_slice_in_dim(padded(spectral_cols[1]), lanes, SPAN)
    base_own = jnp.stack(
        [
            phases(own_left, feat_first, feats // SPAN, D),
            phases(own_right, feat_first, feats // SPAN, D),
        ]
    )

    both = pl.pallas_call(
        spread_kernel,
        in_specs=[VMEM] * 2,
        out_specs=VMEM,
        out_shape=jax.ShapeDtypeStruct((peers_row, own, 2 * feats), BF16),
    )(tokens, cotangent)
    both = exchange(both, PLANE).reshape(count, 2 * feats)

    share = count // peers_z
    half = count // 2
    block = 3 * wide
    smem = pl.BlockSpec(memory_space=pltpu.SMEM)
    hbm = pl.BlockSpec(memory_space=pltpu.HBM)
    anywhere = pl.BlockSpec(memory_space=pl.ANY)
    order = y_index ^ jnp.array([2, 1, 3, 0], jnp.int32)

    def full(shape):
        return pl.BlockSpec(shape, lambda i: (0,) * len(shape))

    table = pl.pallas_call(
        own_table_kernel,
        in_specs=[VMEM],
        out_specs=VMEM,
        out_shape=jax.ShapeDtypeStruct((2, feats, 2 * SPAN), BF16),
        compiler_params=params(8),
    )(base_own)
    def scratch(quarters):
        return [
            pltpu.VMEM((quarters, feats, wide), BF16),
            pltpu.VMEM((quarters, feats, wide), BF16),
            pltpu.VMEM((quarters, wide, feats), BF16),
            pltpu.SemaphoreType.DMA((quarters, 3)),
        ]

    piece = jax.ShapeDtypeStruct((half, block), BF16)
    def swap(value, mask):
        return lax.ppermute(value, "y", [(y, y ^ mask) for y in range(peers_y)])

    early_a, early_b = pl.pallas_call(
        first_kernel,
        in_specs=[smem, VMEM, hbm, hbm, hbm],
        out_specs=[VMEM] * 2,
        out_shape=[piece] * 2,
        scratch_shapes=scratch(1),
        compiler_params=params(52),
    )(order, both, gate_weight, up_weight, down_weight)
    got_early_a, got_early_b = swap(early_a, 1), swap(early_b, 3)
    one, three = pl.pallas_call(
        second_kernel,
        in_specs=[smem, VMEM, hbm, hbm, hbm, VMEM],
        out_specs=[VMEM] * 2,
        out_shape=[jax.ShapeDtypeStruct((count, block), BF16)] * 2,
        scratch_shapes=scratch(2),
        compiler_params=params(52),
    )(order, both, gate_weight, up_weight, down_weight, early_a)
    proj, mine = pl.pallas_call(
        own_kernel,
        in_specs=[smem, VMEM, VMEM, hbm, hbm, hbm, VMEM],
        out_specs=[VMEM] * 2,
        out_shape=[
            jax.ShapeDtypeStruct((count, peers_y * SPAN), BF16),
            jax.ShapeDtypeStruct((count, block), BF16),
        ],
        scratch_shapes=scratch(1),
        compiler_params=params(52),
    )(order, both, table, gate_weight, up_weight, down_weight, one)

    freq, coefs = pl.pallas_call(
        late_kernel,
        in_specs=[VMEM] * 4,
        out_specs=[VMEM] * 2,
        out_shape=[
            jax.ShapeDtypeStruct((4, PAD), jnp.int32),
            jax.ShapeDtypeStruct((2, PAD), F32),
        ],
    )(spectral_rows, spectral_cols, coefficients, one)
    tile_first = unit_first + y_index * wide
    base_up = phases(freq[2], tile_first, wide // SPAN, FF)
    base_down = phases(freq[1], tile_first, wide // SPAN, FF)
    base_out = phases(freq[3], feat_first, feats // SPAN, D)
    sources = (y_index - jnp.arange(peers_y, dtype=jnp.int32)) & 3
    turns = waves(((sources - y_index) * wide)[:, None], freq[1], FF, 1)
    turns = turns.reshape(peers_y, 2, PAD)

    def added(values):
        return pl.pallas_call(
            sum_kernel,
            in_specs=[VMEM] * len(values),
            out_specs=VMEM,
            out_shape=jax.ShapeDtypeStruct(values[0].shape, BF16),
            compiler_params=params(8),
        )(*values)

    def turn(value, axis, peers, k):
        return lax.ppermute(value, axis, [(i, (i + k) % peers) for i in range(peers)])

    one, three, proj = pl.pallas_call(
        fold_kernel,
        in_specs=[VMEM] * 5,
        out_specs=[VMEM] * 3,
        out_shape=[jax.ShapeDtypeStruct((count, block), BF16)] * 2
        + [jax.ShapeDtypeStruct(proj.shape, BF16)],
        compiler_params=params(8),
    )(one, three, got_early_a, got_early_b, proj)
    got_one, got_three = swap(one, 1), swap(three, 3)
    proj = exchange(proj.reshape(peers_z, share, peers_y * SPAN), "z")
    proj = jnp.sum(proj.astype(F32), axis=0).astype(BF16)
    sums, proj = pl.pallas_call(
        close_kernel,
        in_specs=[VMEM] * 4,
        out_specs=[VMEM] * 2,
        out_shape=[
            jax.ShapeDtypeStruct((count, block), BF16),
            jax.ShapeDtypeStruct(proj.shape, BF16),
        ],
        compiler_params=params(8),
    )(mine, got_one, got_three, proj)
    proj = added([proj] + [turn(proj, "y", peers_y, k) for k in (1, 2, 3)])
    proj = jnp.stack([proj, lax.ppermute(proj, "core", [(0, 1), (1, 0)])])
    proj = jnp.stack([proj] + [turn(proj, "x", 4, k) for k in (1, 2, 3)])
    chip = (lax.axis_index("x") - jnp.arange(4, dtype=jnp.int32)) & 3
    core = lax.axis_index("core") ^ jnp.arange(2, dtype=jnp.int32)
    source = jnp.concatenate([chip, core])
    sums = exchange(sums.reshape(peers_z, share, block), "z")

    hidden = pl.pallas_call(
        middle_kernel,
        in_specs=[smem] + [VMEM] * 4,
        out_specs=VMEM,
        out_shape=jax.ShapeDtypeStruct((peers_z, share, wide + SPAN), BF16),
        scratch_shapes=[pltpu.VMEM((2, SPAN, 2 * PAD), BF16)],
        compiler_params=params(12),
    )(source, sums, proj, coefs, jnp.stack([base_up, base_down]))
    def updated(first, after):
        return pl.pallas_call(
            delta_kernel,
            grid=(2,),
            in_specs=[
                smem,
                hbm,
                full(coefs.shape),
                full(base_down.shape),
                full(base_out.shape),
                pl.BlockSpec((1,) + turns.shape[1:], lambda i: (i, 0, 0)),
                anywhere,
            ],
            out_specs=pl.BlockSpec((wide, feats), lambda i: (i, 0)),
            out_shape=jax.ShapeDtypeStruct((2 * wide, feats), BF16),
            scratch_shapes=[
                pltpu.VMEM((wide, 2 * PAD), BF16),
                pltpu.VMEM((2, feats, PAD), F32),
                pltpu.VMEM((feats, 2 * PAD), BF16),
                pltpu.VMEM((2, wide, feats), BF16),
                pltpu.SemaphoreType.DMA((2,)),
            ],
            compiler_params=params(20),
            cost_estimate=pl.CostEstimate(
                flops=4 << 30, bytes_accessed=8 << 20, transcendentals=0
            ),
        )(
            sources[first : first + 2],
            down_weight,
            coefs,
            base_down,
            base_out,
            turns[first : first + 2],
            after,
        )

    near = updated(0, hidden)
    hidden = exchange(hidden, "z")
    hidden = pl.pallas_call(
        regroup_kernel,
        in_specs=[VMEM] * 2,
        out_specs=VMEM,
        out_shape=jax.ShapeDtypeStruct((count + share, wide), BF16),
        compiler_params=params(8),
    )(hidden, near)
    far = updated(2, hidden)
    def shifted(k):
        return lax.ppermute(hidden, "y", [(y, (y + k) % peers_y) for y in range(peers_y)])

    two = shifted(2)
    others = [shifted(1), two, shifted(3)]
    mixed = pl.pallas_call(
        last_kernel,
        in_specs=[VMEM] * 6,
        out_specs=VMEM,
        out_shape=jax.ShapeDtypeStruct((peers_row, 2 * own, feats), BF16),
        compiler_params=params(12),
    )(hidden, *others, near, far)
    mixed = exchange(mixed, PLANE)

    return pl.pallas_call(
        update_kernel,
        in_specs=[VMEM] * 3,
        out_specs=[VMEM] * 2,
        out_shape=[
            jax.ShapeDtypeStruct((own, feats), BF16),
            jax.ShapeDtypeStruct(adam_first.shape, F32),
        ],
        scratch_shapes=[pltpu.VMEM((2, PAD), F32)],
    )(mixed, adam_first, adam_second)


def solution(mesh):
    chips = Mesh(mesh.devices.reshape(4, 2, 8, 4), ("x", "core", "z", "y"))
    tiles = P(("x", "core"), ("z", "y"))
    weights = P(("z", "y"), ("x", "core"))
    placed = (tiles, tiles, weights, weights, tiles, P(), P(), P(), P(), P())
    return jax.shard_map(
        on_device, mesh=chips, in_specs=placed, out_specs=(tiles, P()), check_vma=False
    )
```
